512 devices in a mesh: sky: 32 (over y_hi, z, core), chan: 16 (over x, y_lo).
Axes of the slice: x: 4, y: 8 (y_hi: 2, y_lo: 4; y = y_hi * 4 + y_lo), z: 8, core: 2. Of those that a mesh axis runs over, the one named last changes fastest.
Arguments:
- cube: float32 [16, 768, 8192], P('chan', 'sky')
- noise_weight: float32 [16, 768, 8192], P('chan', 'sky'), may hold values from 0.25 to 4
- spectral_halo: float32 [8, 768, 8192], P(None, 'sky', 'chan'), may hold values from -6 to 6
- source_mask: int32 [768, 8192], P('sky', 'chan'), may hold values from 0 to 1, as said below
- tile_flags: int32 [96, 16], P('sky', 'chan'), may hold values from 0 to 1, as said below
- halo_width: int32 [2, 16], P(None, 'chan'), may hold values from 0 to 4, as said below
Outputs:
- normalized: float32 [3, 16, 768, 8192], P(None, None, 'sky', 'chan')
The draws below stay inside these ranges and needn't reach their ends.
Inputs may be any that keep to these rules, and one draw needn't show every extreme that they name: `halo_width`: in every column of tiles both entries lie in 0 .. 4, and one of them equals 4. `source_mask`: some noise tiles lie wholly in sources. A noise tile whose pixels all have source_mask 1 has tile_flags 0.
All inputs are finite; a program needn't handle non-finite values.
Results may differ from the reference program's by a relative error of at most 0.0001.
Values sent between devices are 32-bit elements; how exact they have to be, the bound alone decides.
No kernel may reach another device: no remote copies, remote signals or barrier semaphores. Data moves between devices by JAX's collectives and lax.ppermute only.
A program may use at most 64 MiB of HBM per device.

```python
import math
import jax
import jax.numpy as jnp
from jax import lax

NX = 8192
RAD = 8
HW = 4
TILE_R = 8
TILE_C = 512
CHANNELS = 16
NY = 768


def draw_cube(key, part):
    key = jax.random.fold_in(key, 3)
    first = jax.random.fold_in(key, 0)
    noise = jax.random.normal(first, (CHANNELS, NY, NX), jnp.float32)
    return noise


def blocked_tiles(key):
    rows_t = NY // TILE_R
    cols_t = NX // TILE_C
    marks = jax.random.randint(key, (rows_t, cols_t), 0, 16) == 0
    chosen = jax.random.randint(jax.random.fold_in(key, 11), (), 0, rows_t * cols_t)
    places = jnp.arange(rows_t * cols_t, dtype=jnp.int32).reshape(rows_t, cols_t)
    return jnp.logical_or(marks, places == chosen)


def draw_source_mask(key, part):
    blocked = blocked_tiles(key)
    key = jax.random.fold_in(key, 5)
    scattered = jax.random.randint(key, (NY, NX), 0, 4) == 0
    spread_out = jnp.repeat(jnp.repeat(blocked, TILE_R, axis=0), TILE_C, axis=1)
    return jnp.logical_or(scattered, spread_out).astype(jnp.int32)


def draw_tile_flags(key, part):
    blocked = blocked_tiles(key)
    key = jax.random.fold_in(key, 9)
    valid = jax.random.randint(key, (NY // TILE_R, NX // TILE_C), 0, 4) != 0
    return jnp.logical_and(valid, jnp.logical_not(blocked)).astype(jnp.int32)


def draw_halo_width(key, part):
    key = jax.random.fold_in(key, 7)
    first, second = jax.random.split(key)
    columns = NX // TILE_C
    side = jax.random.randint(first, (columns,), 0, 2)
    other = jax.random.randint(second, (columns,), 0, HW + 1)
    full = jnp.full((columns,), HW, jnp.int32)
    lower = jnp.where(side == 0, full, other)
    upper = jnp.where(side == 0, other, full)
    return jnp.stack([lower, upper]).astype(jnp.int32)


def steps_of(rng, dims, pieces, smallest, top_value):
    gain, own = 1.0, jax.random.fold_in(rng, 6)
    for dim, parts in pieces:
        draws = jnp.exp(jax.random.uniform(jax.random.fold_in(own, dim), (parts,), jnp.float32, smallest / len(pieces), top_value / len(pieces)))
        gain = gain * jnp.repeat(draws, dims[dim] // parts).reshape([-1 if axis == dim else 1 for axis in range(len(dims))])
    return gain


def gaussian(own_key, dims, scale, bound, pieces=(), kind=jnp.bfloat16):
    level = steps_of(own_key, dims, pieces, -0.22, 0.18) if pieces else 1.0
    array = jax.random.normal(own_key, dims, jnp.float32) * scale * level
    return jnp.minimum(jnp.maximum(array, -bound), bound).astype(kind)


def setup_inputs(seed: int = 0) -> dict:
    keys = jax.random.split(jax.random.key(seed), 7)
    return {
        "cube": draw_cube(jax.random.fold_in(keys[6], 71), 0),
        "noise_weight": jnp.clip(jnp.exp(math.log(4.0) - 2.7725887 * jax.random.uniform(keys[1], (CHANNELS, NY, NX), jnp.float32) ** steps_of(keys[1], (CHANNELS, NY, NX), ((0, 16), (1, 32)), -0.2, 0.2)), 0.25, 4.0),
        "spectral_halo": gaussian(keys[2], (2 * HW, NY, NX), 1.0, 6.0, ((1, 32), (2, 16)), jnp.float32),
        "source_mask": draw_source_mask(jax.random.fold_in(keys[6], 71), 0),
        "tile_flags": draw_tile_flags(jax.random.fold_in(keys[6], 71), 0),
        "halo_width": draw_halo_width(jax.random.fold_in(keys[6], 71), 0),
    }


def tap_list():
    sigma = RAD / 2.5
    return [math.exp(-(shift - RAD) ** 2 / (2.0 * sigma * sigma)) for shift in range(2 * RAD + 1)]

def smooth_along(padded, axis, taps, length):
    total = taps[0] * lax.slice_in_dim(padded, 0, length, axis=axis)
    for shift in range(1, 2 * RAD + 1):
        total = total + taps[shift] * lax.slice_in_dim(padded, shift, shift + length, axis=axis)
    return total

def gauss_plane(values, taps):
    rows, cols = (values.shape[1], values.shape[2])
    padded = jnp.pad(values, ((0, 0), (0, 0), (RAD, RAD)))
    across = smooth_along(padded, 2, taps, cols)
    padded = jnp.pad(across, ((0, 0), (RAD, RAD), (0, 0)))
    return smooth_along(padded, 1, taps, rows)

def reference(cube, noise_weight, spectral_halo, source_mask, tile_flags, halo_width):
    taps = tap_list()
    smoothed = gauss_plane(noise_weight * cube, taps) / gauss_plane(noise_weight, taps)
    channels, rows, cols = smoothed.shape
    place = jnp.arange(HW, dtype=jnp.int32)[:, None]
    lower_keep = (place >= HW - halo_width[0][None, :]).astype(jnp.float32)
    upper_keep = (place < halo_width[1][None, :]).astype(jnp.float32)
    lower_keep = jnp.repeat(lower_keep, TILE_C, axis=1)
    upper_keep = jnp.repeat(upper_keep, TILE_C, axis=1)
    extended = jnp.concatenate([spectral_halo[:HW] * lower_keep[:, None, :], smoothed, spectral_halo[HW:] * upper_keep[:, None, :]], 0)
    keep = (source_mask == 0).astype(jnp.float32)
    tiles_r, tiles_c = (rows // TILE_R, cols // TILE_C)
    count = lax.optimization_barrier(jnp.sum(keep.reshape(tiles_r, TILE_R, tiles_c, TILE_C), axis=(1, 3))) * channels
    flags = tile_flags.astype(jnp.float32)
    results = []
    for width in (3, 5, 9):
        half = width // 2
        boxcar = extended[HW - half:HW - half + channels]
        for shift in range(1, width):
            boxcar = boxcar + extended[HW - half + shift:HW - half + shift + channels]
        boxcar = boxcar / width
        squares = (boxcar * boxcar * keep[None]).reshape(channels, tiles_r, TILE_R, tiles_c, TILE_C)
        total = lax.optimization_barrier(jnp.sum(squares, axis=(0, 2, 4)))
        spread = jnp.sqrt(total / jnp.maximum(count, 1.0) + 1e-06)
        factor = flags / spread
        factor = jnp.repeat(jnp.repeat(factor, TILE_R, axis=0), TILE_C, axis=1)
        results.append(boxcar * factor[None])
    return jnp.stack(results)
```

```python
import functools
import math

import jax
import jax.numpy as jnp
import ml_dtypes
import numpy as np
from jax import lax
from jax.experimental import pallas as pl
from jax.experimental.pallas import tpu as pltpu
from jax.sharding import PartitionSpec as P

RAD = 8
HW = 4
TILE_R = 8
TILE_C = 512
BLK = 256
LANES = 128


def tap_list():
    sigma = RAD / 2.5
    return [math.exp(-((shift - RAD) ** 2) / (2.0 * sigma * sigma)) for shift in range(2 * RAD + 1)]


TAPS = tap_list()[RAD:]


def band_matrices():
    source = np.concatenate([np.arange(BLK), np.arange(-LANES, 0), np.arange(BLK, BLK + LANES)])
    reach = np.abs(source[:, None] - np.arange(BLK)[None, :])
    band = np.where(reach <= RAD, np.asarray(TAPS + [0.0])[np.minimum(reach, RAD + 1)], 0.0)
    high = band.astype(np.float32).astype(ml_dtypes.bfloat16)
    low = (band - high.astype(np.float64)).astype(np.float32).astype(ml_dtypes.bfloat16)
    return np.concatenate([high, high], axis=0), low


def column_taps(tiles):
    count, width = len(tiles), tiles[0].shape[1]
    row = lax.broadcasted_iota(jnp.int32, (TILE_R, width), 0)
    totals = [
        TAPS[RAD] * (tiles[i] + tiles[i + 2]) + TAPS[0] * tiles[i + 1] for i in range(count - 2)
    ]
    for shift in range(1, TILE_R):
        rolled = [pltpu.roll(tile, TILE_R - shift, 0) for tile in tiles]
        joined = [
            jnp.where(row < TILE_R - shift, rolled[i], rolled[i + 1]) for i in range(count - 1)
        ]
        for i in range(count - 2):
            totals[i] = totals[i] + (TAPS[TILE_R - shift] * joined[i] + TAPS[shift] * joined[i + 1])
    return totals


def smooth_kernel(late, side_ref, cube_ref, weight_ref, halo_ref, high_ref, low_ref, out_ref, split):
    side = side_ref[0]
    even = side == 0
    tiles_out = 1 if late else 2
    rows = tiles_out * TILE_R
    blocks = cube_ref.shape[2] // BLK
    split[1, :, BLK : BLK + LANES] = jnp.zeros((2 * rows, LANES), jnp.bfloat16)
    split[1, :, 3 * BLK : 3 * BLK + LANES] = jnp.zeros((2 * rows, LANES), jnp.bfloat16)
    split[blocks, :, BLK + LANES : 2 * BLK] = jnp.zeros((2 * rows, LANES), jnp.bfloat16)
    split[blocks, :, 3 * BLK + LANES :] = jnp.zeros((2 * rows, LANES), jnp.bfloat16)

    def window(ref, halo, cols):
        tile = lambda index: ref[0, pl.ds(pl.multiple_of(index * TILE_R, TILE_R), TILE_R), cols]
        if late:
            middle = tile(1)
            return [jnp.where(even, halo, middle), tile(2 * side), jnp.where(even, middle, halo)]
        return [
            jnp.where(even, tile(0), halo),
            tile(1 - side),
            tile(2 - side),
            jnp.where(even, halo, tile(2)),
        ]

    def rows_step(block, carry):
        cols = pl.ds(pl.multiple_of(block * BLK, BLK), BLK)
        weights = window(weight_ref, halo_ref[1, :, cols], cols)
        values = window(cube_ref, halo_ref[0, :, cols], cols)
        values = [value * weight for value, weight in zip(values, weights)]
        both = jnp.concatenate(column_taps(values) + column_taps(weights), axis=0)
        high = both.astype(jnp.bfloat16)
        low = (both - high.astype(jnp.float32)).astype(jnp.bfloat16)
        for part, base in ((high, 0), (low, 2 * BLK)):
            split[block + 1, :, base : base + BLK] = part
            split[block + 2, :, base + BLK : base + BLK + LANES] = part[:, LANES:]
            split[block, :, base + BLK + LANES : base + 2 * BLK] = part[:, :LANES]
        return carry

    lax.fori_loop(0, blocks, rows_step, 0)

    group = 8 if late else 4

    def columns_step(step, carry):
        part = split[pl.ds(step * group + 1, group)].reshape(group * 2 * rows, 4 * BLK)
        both = jnp.dot(part, high_ref[...], preferred_element_type=jnp.float32)
        both += jnp.dot(part[:, : 2 * BLK], low_ref[...], preferred_element_type=jnp.float32)
        both = both.reshape(group, 2 * rows, BLK)
        ratio = both[:, :rows] / both[:, rows:]
        for i in range(group):
            out_ref[step * (group // 2) + i // 2, :, (i % 2) * BLK : (i % 2 + 1) * BLK] = ratio[i]
        return carry

    lax.fori_loop(0, blocks // group, columns_step, 0)


def smooth_rows(late, side, cube, weight, halo, high, low):
    rows = TILE_R if late else 2 * TILE_R
    columns = cube.shape[2]
    blocks = columns // BLK
    whole = pl.BlockSpec(memory_space=pltpu.VMEM)
    return pl.pallas_call(
        functools.partial(smooth_kernel, late),
        out_shape=jax.ShapeDtypeStruct((columns // TILE_C, rows, TILE_C), jnp.float32),
        in_specs=[pl.BlockSpec(memory_space=pltpu.SMEM)] + [whole] * 5,
        out_specs=whole,
        scratch_shapes=[pltpu.VMEM((blocks + 2, 2 * rows, 4 * BLK), jnp.bfloat16)],
        compiler_params=pltpu.CompilerParams(vmem_limit_bytes=24 * 1024 * 1024),
        cost_estimate=pl.CostEstimate(
            flops=4 * rows * columns * 2 * BLK, bytes_accessed=16 * rows * columns, transcendentals=0
        ),
    )(side, cube, weight, halo, high, low)


def norm_kernel(base, tiles_ref, smooth_ref, halo_ref, mask_ref, flags_ref, width_ref, *rest):
    out_ref = rest[-1]
    channels = smooth_ref.shape[0]
    tile = tiles_ref[0] + pl.program_id(0)
    keep_low = [(j >= HW - width_ref[0, 0]).astype(jnp.float32) for j in range(HW)]
    keep_high = [(j < width_ref[1, 0]).astype(jnp.float32) for j in range(HW)]
    sums = [jnp.zeros((TILE_R, LANES), jnp.float32) for _ in range(3)]
    kept = jnp.zeros((TILE_R, LANES), jnp.float32)
    for strip in range(TILE_C // LANES):
        cols = slice(strip * LANES, (strip + 1) * LANES)
        keep = (mask_ref[:, cols] == 0).astype(jnp.float32)
        kept = kept + keep
        extended = [halo_ref[j, :, cols] * keep_low[j] for j in range(HW)]
        extended += [smooth_ref[c, :, cols] for c in range(channels)]
        extended += [halo_ref[HW + j, :, cols] * keep_high[j] for j in range(HW)]
        squares = [jnp.zeros((TILE_R, LANES), jnp.float32) for _ in range(3)]
        for c in range(channels):
            at = c + HW
            three = extended[at - 1] + extended[at] + extended[at + 1]
            five = three + (extended[at - 2] + extended[at + 2])
            nine = five + ((extended[at - 3] + extended[at + 3]) + (extended[at - 4] + extended[at + 4]))
            for i, (total, width) in enumerate(((three, 3), (five, 5), (nine, 9))):
                boxcar = total * (1.0 / width)
                out_ref[i, c, :, cols] = boxcar
                squares[i] = squares[i] + boxcar * boxcar
        sums = [total + square * keep for total, square in zip(sums, squares)]

    def whole(x):
        return jnp.sum(jnp.sum(x, axis=1, keepdims=True), axis=0, keepdims=True)

    count = jnp.maximum(whole(kept) * channels, 1.0)
    flag = flags_ref[tile, 0].astype(jnp.float32)
    for i in range(3):
        factor = flag / jnp.sqrt(whole(sums[i]) / count + 1e-06)
        factor = jnp.broadcast_to(factor, (TILE_R, TILE_C))
        for c in range(channels):
            out_ref[i, c] = out_ref[i, c] * factor


def normalize(first, smoothed, halo, mask, flags, widths, before=None):
    channels, rows, columns = smoothed.shape
    steps = rows // TILE_R
    out = jax.ShapeDtypeStruct((3, channels) + mask.shape, jnp.float32)
    in_specs = [
        pl.BlockSpec((channels, TILE_R, columns), lambda i, at: (0, i, 0)),
        pl.BlockSpec((2 * HW, TILE_R, columns), lambda i, at: (0, at[0] + i, 0)),
        pl.BlockSpec((TILE_R, columns), lambda i, at: (at[0] + i, 0)),
        pl.BlockSpec(memory_space=pltpu.SMEM),
        pl.BlockSpec(memory_space=pltpu.SMEM),
    ]
    operands = [first, smoothed, halo, mask, flags, widths]
    aliases = {}
    if before is not None:
        in_specs.append(pl.BlockSpec(memory_space=pl.ANY))
        operands.append(before)
        aliases = {6: 0}
    return pl.pallas_call(
        functools.partial(norm_kernel, None),
        out_shape=out,
        grid_spec=pltpu.PrefetchScalarGridSpec(
            num_scalar_prefetch=1,
            grid=(steps,),
            in_specs=in_specs,
            out_specs=pl.BlockSpec(
                (3, channels, TILE_R, columns), lambda i, at: (0, 0, at[0] + i, 0)
            ),
        ),
        input_output_aliases=aliases,
        compiler_params=pltpu.CompilerParams(vmem_limit_bytes=16 * 1024 * 1024),
        cost_estimate=pl.CostEstimate(
            flops=30 * smoothed.size, bytes_accessed=20 * smoothed.size, transcendentals=0
        ),
    )(*operands)


def local(cube, noise_weight, spectral_halo, source_mask, tile_flags, halo_width):
    high, low = (jnp.asarray(part) for part in band_matrices())
    sky = lax.axis_size("sky")
    side = lax.axis_index("sky") % 2
    last = cube.shape[1] - TILE_R
    near = [(i, i ^ 1) for i in range(sky)]
    far = [(i, i + 1) for i in range(1, sky - 1, 2)]
    far = far + [(target, source) for source, target in far]

    def edge(start):
        return jnp.concatenate(
            [lax.dynamic_slice_in_dim(part, start, TILE_R, axis=1) for part in (cube, noise_weight)], axis=0
        )

    far_halo = lax.ppermute(edge(side * last), "sky", far)
    near_halo = lax.ppermute(edge((1 - side) * last), "sky", near)
    sides = jnp.reshape(side, (1,))
    early = smooth_rows(False, sides, cube, noise_weight, near_halo, high, low)
    early = lax.all_to_all(early, "chan", split_axis=0, concat_axis=0, tiled=True)
    late = smooth_rows(True, sides, cube, noise_weight, far_halo, high, low)
    late = lax.all_to_all(late, "chan", split_axis=0, concat_axis=0, tiled=True)
    rest = (spectral_halo, source_mask, tile_flags, halo_width)
    result = normalize(1 - sides, early, *rest)
    return normalize(2 * sides, late, *rest, before=result)


def solution(mesh):
    placed = (
        P("chan", "sky", None),
        P("chan", "sky", None),
        P(None, "sky", "chan"),
        P("sky", "chan"),
        P("sky", "chan"),
        P(None, "chan"),
    )
    return jax.shard_map(
        local, mesh=mesh, in_specs=placed, out_specs=P(None, None, "sky", "chan"), check_vma=False
    )
```

```python
import functools
import math

import jax
import jax.numpy as jnp
from jax import lax
from jax.experimental import pallas as pl
from jax.experimental.pallas import tpu as pltpu
from jax.sharding import PartitionSpec as P

RAD = 8
HW = 4
TILE_R = 8
TILE_C = 512
BLK = 256
LANES = 128
CHUNKS = 4


def tap_list():
    sigma = RAD / 2.5
    return [math.exp(-((shift - RAD) ** 2) / (2.0 * sigma * sigma)) for shift in range(2 * RAD + 1)]


TAPS = tap_list()[RAD:]


def band_matrices(high_ref, low_ref):
    shape = (LANES, BLK)
    target = lax.broadcasted_iota(jnp.int32, shape, 1)
    for part, first in enumerate((0, LANES, -LANES, BLK)):
        reach = jnp.abs(lax.broadcasted_iota(jnp.int32, shape, 0) + first - target)
        band = jnp.zeros(shape, jnp.float32)
        for shift in range(RAD + 1):
            band = jnp.where(reach == shift, TAPS[shift], band)
        high = band.astype(jnp.bfloat16)
        rows = slice(part * LANES, (part + 1) * LANES)
        high_ref[rows] = high
        low_ref[rows] = (band - high.astype(jnp.float32)).astype(jnp.bfloat16)


def column_taps(tiles):
    count, width = len(tiles), tiles[0].shape[1]
    row = lax.broadcasted_iota(jnp.int32, (TILE_R, width), 0)
    totals = [
        TAPS[RAD] * (tiles[i] + tiles[i + 2]) + TAPS[0] * tiles[i + 1] for i in range(count - 2)
    ]
    for shift in range(1, TILE_R):
        rolled = [pltpu.roll(tile, TILE_R - shift, 0) for tile in tiles]
        joined = [
            jnp.where(row < TILE_R - shift, rolled[i], rolled[i + 1]) for i in range(count - 1)
        ]
        for i in range(count - 2):
            totals[i] = totals[i] + (TAPS[TILE_R - shift] * joined[i] + TAPS[shift] * joined[i + 1])
    return totals


def smooth_kernel(
    late, side_ref, cube_ref, weight_ref, halo_ref, out_hbm, split, lines, high_ref, low_ref, out_ref, sent
):
    side = side_ref[0]
    even = side == 0
    tiles_out = 1 if late else 2
    rows = tiles_out * TILE_R
    blocks = cube_ref.shape[2] // BLK
    band_matrices(high_ref, low_ref)
    split[1, :, BLK : BLK + LANES] = jnp.zeros((2 * rows, LANES), jnp.bfloat16)
    split[1, :, 3 * BLK : 3 * BLK + LANES] = jnp.zeros((2 * rows, LANES), jnp.bfloat16)
    split[blocks, :, BLK + LANES : 2 * BLK] = jnp.zeros((2 * rows, LANES), jnp.bfloat16)
    split[blocks, :, 3 * BLK + LANES :] = jnp.zeros((2 * rows, LANES), jnp.bfloat16)

    def window(ref, halo, cols):
        tile = lambda index: ref[0, pl.ds(pl.multiple_of(index * TILE_R, TILE_R), TILE_R), cols]
        if late:
            middle = tile(1)
            return [jnp.where(even, halo, middle), tile(2 * side), jnp.where(even, middle, halo)]
        return [
            jnp.where(even, tile(0), halo),
            tile(1 - side),
            tile(2 - side),
            jnp.where(even, halo, tile(2)),
        ]

    def rows_step(block, carry):
        cols = pl.ds(pl.multiple_of(block * BLK, BLK), BLK)
        weights = window(weight_ref, halo_ref[1, :, cols], cols)
        values = window(cube_ref, halo_ref[0, :, cols], cols)
        values = [value * weight for value, weight in zip(values, weights)]
        sides = []
        for slot, half in enumerate((0, LANES)):
            for kind, tiles in enumerate((values, weights)):
                at = 2 * slot + kind
                for i, tile in enumerate(tiles):
                    lines[at, TILE_R * i : TILE_R * (i + 1)] = tile[:, half : half + LANES]
        for slot in range(2):
            made = []
            for kind in range(2):
                at = 2 * slot + kind
                line = lambda start: lines[at, start : start + rows]
                total = TAPS[0] * line(RAD)
                for shift in range(1, RAD + 1):
                    total = total + TAPS[shift] * (line(RAD - shift) + line(RAD + shift))
                made.append(total)
            sides.append(jnp.concatenate(made, axis=0))
        both = jnp.concatenate(sides, axis=1)
        high = both.astype(jnp.bfloat16)
        low = (both - high.astype(jnp.float32)).astype(jnp.bfloat16)
        for part, base in ((high, 0), (low, 2 * BLK)):
            split[block + 1, :, base : base + BLK] = part
            split[block + 2, :, base + BLK : base + BLK + LANES] = part[:, LANES:]
            split[block, :, base + BLK + LANES : base + 2 * BLK] = part[:, :LANES]
        return carry

    lax.fori_loop(0, blocks, rows_step, 0, unroll=2)
    group = blocks // CHUNKS
    parts = []
    for step in range(CHUNKS):
        part = split[step * group + 1 : (step + 1) * group + 1].reshape(group * 2 * rows, 4 * BLK)
        both = jnp.dot(part[:, : 2 * BLK], high_ref[...], preferred_element_type=jnp.float32)
        both += jnp.dot(part[:, 2 * BLK :], high_ref[...], preferred_element_type=jnp.float32)
        both += jnp.dot(part[:, : 2 * BLK], low_ref[...], preferred_element_type=jnp.float32)
        both = both.reshape(group, 2 * rows, BLK)
        ratio = both[:, :rows] / both[:, rows:]
        first = step * (group // 2)
        for i in range(group):
            out_ref[first + i // 2, :, (i % 2) * BLK : (i % 2 + 1) * BLK] = ratio[i]
        piece = pl.ds(first, group // 2)
        parts.append(pltpu.make_async_copy(out_ref.at[piece], out_hbm.at[piece], sent.at[step]))
        parts[-1].start()
    for copy in parts:
        copy.wait()


def edge_kernel(side_ref, cube_ref, weight_ref, far_ref, near_ref, done):
    side = side_ref[0]
    last = cube_ref.shape[1] - TILE_R
    copies = []
    for k, (out_ref, start) in enumerate(((far_ref, side * last), (near_ref, (1 - side) * last))):
        rows = pl.ds(pl.multiple_of(start, TILE_R), TILE_R)
        for j, ref in enumerate((cube_ref, weight_ref)):
            copies.append(
                pltpu.make_async_copy(ref.at[0, rows], out_ref.at[j], done.at[2 * k + j])
            )
    for copy in copies:
        copy.start()
    for copy in copies:
        copy.wait()


def edge_rows(side, cube, weight):
    edge = pltpu.VMEM((2, TILE_R, cube.shape[2]), cube.dtype)
    whole = pl.BlockSpec(memory_space=pltpu.VMEM)
    return pl.pallas_call(
        edge_kernel,
        out_shape=[edge, edge],
        in_specs=[pl.BlockSpec(memory_space=pltpu.SMEM)] + [pl.BlockSpec(memory_space=pl.ANY)] * 2,
        out_specs=[whole, whole],
        scratch_shapes=[pltpu.SemaphoreType.DMA((4,))],
        compiler_params=pltpu.CompilerParams(vmem_limit_bytes=8 * 1024 * 1024),
        cost_estimate=pl.CostEstimate(
            flops=10**11, bytes_accessed=64 * TILE_R * cube.shape[2], transcendentals=0
        ),
    )(side, cube, weight)


def smooth_rows(late, side, cube, weight, halo):
    rows = TILE_R if late else 2 * TILE_R
    columns = cube.shape[2]
    blocks = columns // BLK
    whole = pl.BlockSpec(memory_space=pltpu.VMEM)
    return pl.pallas_call(
        functools.partial(smooth_kernel, late),
        out_shape=pltpu.HBM((columns // TILE_C, rows, TILE_C), jnp.float32),
        in_specs=[pl.BlockSpec(memory_space=pltpu.SMEM)] + [whole] * 3,
        out_specs=pl.BlockSpec(memory_space=pl.ANY),
        scratch_shapes=[pltpu.VMEM((blocks + 2, 2 * rows, 4 * BLK), jnp.bfloat16), pltpu.VMEM((4, rows + 2 * TILE_R, LANES), jnp.float32),
            pltpu.VMEM((2 * BLK, BLK), jnp.bfloat16),
            pltpu.VMEM((2 * BLK, BLK), jnp.bfloat16),
            pltpu.VMEM((columns // TILE_C, rows, TILE_C), jnp.float32),
            pltpu.SemaphoreType.DMA((CHUNKS,)),
        ],
        compiler_params=pltpu.CompilerParams(vmem_limit_bytes=24 * 1024 * 1024),
        cost_estimate=pl.CostEstimate(
            flops=10**11, bytes_accessed=16 * rows * columns, transcendentals=0
        ),
    )(side, cube, weight, halo)


def norm_kernel(tiles_ref, smooth_ref, halo_ref, mask_ref, flags_ref, width_ref, *rest):
    out_ref = rest[-1]
    channels = smooth_ref.shape[0]
    tile = tiles_ref[0] + pl.program_id(0)
    keep_low = [(j >= HW - width_ref[0, 0]).astype(jnp.float32) for j in range(HW)]
    keep_high = [(j < width_ref[1, 0]).astype(jnp.float32) for j in range(HW)]
    sums = [jnp.zeros((TILE_R, LANES), jnp.float32) for _ in range(3)]
    kept = jnp.zeros((TILE_R, LANES), jnp.float32)
    for strip in range(TILE_C // LANES):
        cols = slice(strip * LANES, (strip + 1) * LANES)
        keep = (mask_ref[:, cols] == 0).astype(jnp.float32)
        kept = kept + keep
        extended = [halo_ref[j, :, cols] * keep_low[j] for j in range(HW)]
        extended += [smooth_ref[c, :, cols] for c in range(channels)]
        extended += [halo_ref[HW + j, :, cols] * keep_high[j] for j in range(HW)]
        squares = [jnp.zeros((TILE_R, LANES), jnp.float32) for _ in range(3)]
        for c in range(channels):
            at = c + HW
            three = extended[at - 1] + extended[at] + extended[at + 1]
            five = three + (extended[at - 2] + extended[at + 2])
            nine = five + ((extended[at - 3] + extended[at + 3]) + (extended[at - 4] + extended[at + 4]))
            for i, (total, width) in enumerate(((three, 3), (five, 5), (nine, 9))):
                boxcar = total * (1.0 / width)
                out_ref[i, c, :, cols] = boxcar
                squares[i] = squares[i] + boxcar * boxcar
        sums = [total + square * keep for total, square in zip(sums, squares)]

    def whole(x):
        return jnp.sum(jnp.sum(x, axis=1, keepdims=True), axis=0, keepdims=True)

    count = jnp.maximum(whole(kept) * channels, 1.0)
    flag = flags_ref[tile, 0].astype(jnp.float32)
    for i in range(3):
        factor = flag / jnp.sqrt(whole(sums[i]) / count + 1e-06)
        factor = jnp.broadcast_to(factor, (TILE_R, TILE_C))
        for c in range(channels):
            out_ref[i, c] = out_ref[i, c] * factor


def normalize(first, smoothed, halo, mask, flags, widths, before=None):
    channels, rows, columns = smoothed.shape
    steps = rows // TILE_R
    out = jax.ShapeDtypeStruct((3, channels) + mask.shape, jnp.float32)
    in_specs = [
        pl.BlockSpec((channels, TILE_R, columns), lambda i, at: (0, i, 0)),
        pl.BlockSpec((2 * HW, TILE_R, columns), lambda i, at: (0, at[0] + i, 0)),
        pl.BlockSpec((TILE_R, columns), lambda i, at: (at[0] + i, 0)),
        pl.BlockSpec(memory_space=pltpu.SMEM),
        pl.BlockSpec(memory_space=pltpu.SMEM),
    ]
    operands = [first, smoothed, halo, mask, flags, widths]
    aliases = {}
    if before is not None:
        in_specs.append(pl.BlockSpec(memory_space=pl.ANY))
        operands.append(before)
        aliases = {6: 0}
    return pl.pallas_call(
        norm_kernel,
        out_shape=out,
        grid_spec=pltpu.PrefetchScalarGridSpec(
            num_scalar_prefetch=1,
            grid=(steps,),
            in_specs=in_specs,
            out_specs=pl.BlockSpec(
                (3, channels, TILE_R, columns), lambda i, at: (0, 0, at[0] + i, 0)
            ),
        ),
        input_output_aliases=aliases,
        compiler_params=pltpu.CompilerParams(vmem_limit_bytes=16 * 1024 * 1024),
        cost_estimate=pl.CostEstimate(
            flops=30 * smoothed.size, bytes_accessed=20 * smoothed.size, transcendentals=0
        ),
    )(*operands)


def local(cube, noise_weight, spectral_halo, source_mask, tile_flags, halo_width):
    sky = lax.axis_size("sky")
    side = lax.axis_index("sky") & 1
    near = [(i, i ^ 1) for i in range(sky)]
    far = [(i, i + 1) for i in range(1, sky - 1, 2)]
    far = far + [(target, source) for source, target in far]

    sides = jnp.reshape(side, (1,))
    stay = [pltpu.with_memory_space_constraint(part, pltpu.HBM) for part in (cube, noise_weight)]
    far_edge, near_edge = edge_rows(sides, *stay)
    far_halo = lax.ppermute(far_edge, "sky", far)
    near_halo = lax.ppermute(near_edge, "sky", near)
    early = smooth_rows(False, sides, cube, noise_weight, near_halo)
    early = lax.all_to_all(early, "chan", split_axis=0, concat_axis=0, tiled=True)
    far_halo = pltpu.with_memory_space_constraint(far_halo, pltpu.VMEM)
    late = smooth_rows(True, sides, cube, noise_weight, far_halo)
    late = lax.all_to_all(late, "chan", split_axis=0, concat_axis=0, tiled=True)
    rest = (spectral_halo, source_mask, tile_flags, halo_width)
    result = normalize(1 - sides, early, *rest)
    return normalize(2 * sides, late, *rest, before=result)


def solution(mesh):
    placed = (
        P("chan", "sky", None),
        P("chan", "sky", None),
        P(None, "sky", "chan"),
        P("sky", "chan"),
        P("sky", "chan"),
        P(None, "chan"),
    )
    return jax.shard_map(
        local, mesh=mesh, in_specs=placed, out_specs=P(None, None, "sky", "chan"), check_vma=False
    )
```

```python
import functools
import math

import jax
import jax.numpy as jnp
from jax import lax
from jax.experimental import pallas as pl
from jax.experimental.pallas import tpu as pltpu
from jax.sharding import PartitionSpec as P

RAD = 8
HW = 4
TILE_R = 8
TILE_C = 512
BLK = 256
LANES = 128
CHUNKS = 4
WIDTHS = (3, 5, 9)


def tap_list():
    sigma = RAD / 2.5
    return [math.exp(-((shift - RAD) ** 2) / (2.0 * sigma * sigma)) for shift in range(2 * RAD + 1)]


TAPS = tap_list()[RAD:]


def band_matrices(high_ref, low_ref):
    shape = (LANES, BLK)
    target = lax.broadcasted_iota(jnp.int32, shape, 1)
    for part, first in enumerate((0, LANES, -LANES, BLK)):
        reach = jnp.abs(lax.broadcasted_iota(jnp.int32, shape, 0) + first - target)
        band = jnp.zeros(shape, jnp.float32)
        for shift in range(RAD + 1):
            band = jnp.where(reach == shift, TAPS[shift], band)
        high = band.astype(jnp.bfloat16)
        rows = slice(part * LANES, (part + 1) * LANES)
        high_ref[rows] = high
        low_ref[rows] = (band - high.astype(jnp.float32)).astype(jnp.bfloat16)


def column_taps(tiles):
    count, width = len(tiles), tiles[0].shape[1]
    row = lax.broadcasted_iota(jnp.int32, (TILE_R, width), 0)
    totals = [
        TAPS[RAD] * (tiles[i] + tiles[i + 2]) + TAPS[0] * tiles[i + 1] for i in range(count - 2)
    ]
    for shift in range(1, TILE_R):
        rolled = [pltpu.roll(tile, TILE_R - shift, 0) for tile in tiles]
        joined = [
            jnp.where(row < TILE_R - shift, rolled[i], rolled[i + 1]) for i in range(count - 1)
        ]
        for i in range(count - 2):
            totals[i] = totals[i] + (TAPS[TILE_R - shift] * joined[i] + TAPS[shift] * joined[i + 1])
    return totals


def smooth_kernel(
    late, side_ref, cube_ref, weight_ref, *rest
):
    out_hbm, split, lines, high_ref, low_ref, out_ref, sent = rest[-7:]
    halos = rest[:-8] if late else rest[:-7]
    side = side_ref[0] & 1
    even = side == 0
    border = side_ref[0] > 1
    tiles_out = 1 if late else 2
    rows = tiles_out * TILE_R
    blocks = cube_ref.shape[2] // BLK
    band_matrices(high_ref, low_ref)
    split[1, :, BLK : BLK + LANES] = jnp.zeros((2 * rows, LANES), jnp.bfloat16)
    split[1, :, 3 * BLK : 3 * BLK + LANES] = jnp.zeros((2 * rows, LANES), jnp.bfloat16)
    split[blocks, :, BLK + LANES : 2 * BLK] = jnp.zeros((2 * rows, LANES), jnp.bfloat16)
    split[blocks, :, 3 * BLK + LANES :] = jnp.zeros((2 * rows, LANES), jnp.bfloat16)

    def window(ref, halo, cols):
        tile = lambda index: ref[0, pl.ds(pl.multiple_of(index * TILE_R, TILE_R), TILE_R), cols]
        if late:
            middle = tile(1)
            return [jnp.where(even, halo, middle), tile(2 * side), jnp.where(even, middle, halo)]
        return [
            jnp.where(even, tile(0), halo),
            tile(1 - side),
            tile(2 - side),
            jnp.where(even, halo, tile(2)),
        ]

    def rows_step(block, carry):
        cols = pl.ds(pl.multiple_of(block * BLK, BLK), BLK)
        cube_halo, weight_halo = halos[0][0, :, cols], halos[0][1, :, cols]
        if not late:
            cube_halo = jnp.where(border, cube_halo, halos[1][:, cols])
            weight_halo = jnp.where(border, weight_halo, halos[2][:, cols])
        weights = window(weight_ref, weight_halo, cols)
        values = window(cube_ref, cube_halo, cols)
        values = [value * weight for value, weight in zip(values, weights)]
        sides = []
        for slot, half in enumerate((0, LANES)):
            for kind, tiles in enumerate((values, weights)):
                at = 2 * slot + kind
                for i, tile in enumerate(tiles):
                    lines[at, TILE_R * i : TILE_R * (i + 1)] = tile[:, half : half + LANES]
        for slot in range(2):
            made = []
            for kind in range(2):
                at = 2 * slot + kind
                line = lambda start: lines[at, start : start + rows]
                total = TAPS[0] * line(RAD)
                for shift in range(1, RAD + 1):
                    total = total + TAPS[shift] * (line(RAD - shift) + line(RAD + shift))
                made.append(total)
            sides.append(jnp.concatenate(made, axis=0))
        both = jnp.concatenate(sides, axis=1)
        high = both.astype(jnp.bfloat16)
        low = (both - high.astype(jnp.float32)).astype(jnp.bfloat16)
        for part, base in ((high, 0), (low, 2 * BLK)):
            split[block + 1, :, base : base + BLK] = part
            split[block + 2, :, base + BLK : base + BLK + LANES] = part[:, LANES:]
            split[block, :, base + BLK + LANES : base + 2 * BLK] = part[:, :LANES]
        return carry

    lax.fori_loop(0, blocks, rows_step, 0, unroll=2)
    group = blocks // CHUNKS
    top = pl.multiple_of((2 * side if late else 1 - side) * TILE_R, TILE_R)
    parts = []
    for step in range(CHUNKS):
        part = split[step * group + 1 : (step + 1) * group + 1].reshape(group * 2 * rows, 4 * BLK)
        both = jnp.dot(part[:, : 2 * BLK], high_ref[...], preferred_element_type=jnp.float32)
        both += jnp.dot(part[:, 2 * BLK :], high_ref[...], preferred_element_type=jnp.float32)
        both += jnp.dot(part[:, : 2 * BLK], low_ref[...], preferred_element_type=jnp.float32)
        both = both.reshape(group, 2 * rows, BLK)
        ratio = both[:, :rows] / both[:, rows:]
        first = step * (group // 2)
        for i in range(group):
            out_ref[first + i // 2, :, (i % 2) * BLK : (i % 2 + 1) * BLK] = ratio[i]
        piece = pl.ds(first, group // 2)
        place = out_hbm.at[piece, pl.ds(top, rows)]
        parts.append(pltpu.make_async_copy(out_ref.at[piece], place, sent.at[step]))
        parts[-1].start()
    for copy in parts:
        copy.wait()


def edge_kernel(side_ref, cube_ref, weight_ref, far_ref, near_ref, done):
    side = side_ref[0] & 1
    last = cube_ref.shape[1] - TILE_R
    copies = []
    for k, (out_ref, start) in enumerate(((far_ref, side * last), (near_ref, (1 - side) * last))):
        rows = pl.ds(pl.multiple_of(start, TILE_R), TILE_R)
        for j, ref in enumerate((cube_ref, weight_ref)):
            copies.append(
                pltpu.make_async_copy(ref.at[0, rows], out_ref.at[j], done.at[2 * k + j])
            )
    for copy in copies:
        copy.start()
    for copy in copies:
        copy.wait()


def edge_rows(side, cube, weight):
    edge = pltpu.VMEM((2, TILE_R, cube.shape[2]), cube.dtype)
    whole = pl.BlockSpec(memory_space=pltpu.VMEM)
    return pl.pallas_call(
        edge_kernel,
        out_shape=[edge, edge],
        in_specs=[pl.BlockSpec(memory_space=pltpu.SMEM)] + [pl.BlockSpec(memory_space=pl.ANY)] * 2,
        out_specs=[whole, whole],
        scratch_shapes=[pltpu.SemaphoreType.DMA((4,))],
        compiler_params=pltpu.CompilerParams(vmem_limit_bytes=8 * 1024 * 1024),
        cost_estimate=pl.CostEstimate(
            flops=10**11, bytes_accessed=64 * TILE_R * cube.shape[2], transcendentals=0
        ),
    )(side, cube, weight)


def smooth_rows(side, cube, weight, *halo, before=None):
    late = before is not None
    rows = TILE_R if late else 2 * TILE_R
    columns = cube.shape[2]
    blocks = columns // BLK
    whole = pl.BlockSpec(memory_space=pltpu.VMEM)
    return pl.pallas_call(
        functools.partial(smooth_kernel, late),
        out_shape=pltpu.HBM((columns // TILE_C, cube.shape[1], TILE_C), jnp.float32),
        in_specs=[pl.BlockSpec(memory_space=pltpu.SMEM)] + [whole] * (2 + len(halo)) + [pl.BlockSpec(memory_space=pl.ANY)] * late,
        out_specs=pl.BlockSpec(memory_space=pl.ANY),
        input_output_aliases={4: 0} if late else {},
        scratch_shapes=[pltpu.VMEM((blocks + 2, 2 * rows, 4 * BLK), jnp.bfloat16), pltpu.VMEM((4, rows + 2 * TILE_R, LANES), jnp.float32),
            pltpu.VMEM((2 * BLK, BLK), jnp.bfloat16),
            pltpu.VMEM((2 * BLK, BLK), jnp.bfloat16),
            pltpu.VMEM((columns // TILE_C, rows, TILE_C), jnp.float32),
            pltpu.SemaphoreType.DMA((CHUNKS,)),
        ],
        compiler_params=pltpu.CompilerParams(vmem_limit_bytes=24 * 1024 * 1024),
        cost_estimate=pl.CostEstimate(
            flops=4 * rows * columns * 2 * BLK, bytes_accessed=16 * rows * columns, transcendentals=0
        ),
    )(side, cube, weight, *halo, *([before] if late else []))


def norm_kernel(smooth_ref, halo_ref, mask_ref, flags_ref, width_ref, out_hbm, out_ref, sent):
    channels, rows, columns = smooth_ref.shape
    keep_low = [(j >= HW - width_ref[0, 0]).astype(jnp.float32) for j in range(HW)]
    keep_high = [(j < width_ref[1, 0]).astype(jnp.float32) for j in range(HW)]

    def whole(x):
        return jnp.sum(jnp.sum(x, axis=1, keepdims=True), axis=0, keepdims=True)

    copies = []
    for tile in range(rows // TILE_R):
        lines = slice(tile * TILE_R, (tile + 1) * TILE_R)
        sums = [jnp.zeros((TILE_R, LANES), jnp.float32) for _ in WIDTHS]
        kept = jnp.zeros((TILE_R, LANES), jnp.float32)
        for strip in range(columns // LANES):
            cols = slice(strip * LANES, (strip + 1) * LANES)
            keep = (mask_ref[lines, cols] == 0).astype(jnp.float32)
            kept = kept + keep
            extended = [halo_ref[j, lines, cols] * keep_low[j] for j in range(HW)]
            extended += [smooth_ref[c, lines, cols] for c in range(channels)]
            extended += [halo_ref[HW + j, lines, cols] * keep_high[j] for j in range(HW)]
            squares = [jnp.zeros((TILE_R, LANES), jnp.float32) for _ in WIDTHS]
            for c in range(channels):
                at = c + HW
                total = extended[at]
                reach = 0
                for i, width in enumerate(WIDTHS):
                    while reach < width // 2:
                        reach += 1
                        total = total + (extended[at - reach] + extended[at + reach])
                    boxcar = total * (1.0 / width)
                    out_ref[i, c, lines, cols] = boxcar
                    squares[i] = squares[i] + boxcar * boxcar
            sums = [total + square * keep for total, square in zip(sums, squares)]
        count = jnp.maximum(whole(kept) * channels, 1.0)
        flag = flags_ref[tile, 0].astype(jnp.float32)
        for i in range(len(WIDTHS)):
            factor = flag / jnp.sqrt(whole(sums[i]) / count + 1e-06)
            factor = jnp.broadcast_to(factor, (TILE_R, columns))
            for c in range(channels):
                out_ref[i, c, lines] = out_ref[i, c, lines] * factor
            copies.append(
                pltpu.make_async_copy(out_ref.at[i, :, lines], out_hbm.at[i, :, lines], sent.at[tile, i])
            )
            copies[-1].start()
    for copy in copies:
        copy.wait()


def normalize(smoothed, halo, mask, flags, widths):
    out = (len(WIDTHS),) + smoothed.shape
    whole = pl.BlockSpec(memory_space=pltpu.VMEM)
    scalars = pl.BlockSpec(memory_space=pltpu.SMEM)
    return pl.pallas_call(
        norm_kernel,
        out_shape=jax.ShapeDtypeStruct(out, jnp.float32),
        in_specs=[whole, whole, whole, scalars, scalars],
        out_specs=pl.BlockSpec(memory_space=pl.ANY),
        scratch_shapes=[
            pltpu.VMEM(out, jnp.float32),
            pltpu.SemaphoreType.DMA((smoothed.shape[1] // TILE_R, len(WIDTHS))),
        ],
        compiler_params=pltpu.CompilerParams(vmem_limit_bytes=16 * 1024 * 1024),
        cost_estimate=pl.CostEstimate(
            flops=30 * smoothed.size, bytes_accessed=20 * smoothed.size, transcendentals=0
        ),
    )(smoothed, halo, mask, flags, widths)


def local(cube, noise_weight, spectral_halo, source_mask, tile_flags, halo_width):
    sky = lax.axis_size("sky")
    place = lax.axis_index("sky")
    side = place & 1
    half = sky // 2
    border = [(half, half + 1), (half + 1, half)]
    near = [(i, i ^ 1) for i in range(sky) if (i, i ^ 1) not in border]
    far = [(i, i + 1) for i in range(1, sky - 1, 2)]
    far = far + [(target, source) for source, target in far]
    sides = jnp.reshape(side + 2 * (place // 2 == half // 2).astype(jnp.int32), (1,))
    stay = [pltpu.with_memory_space_constraint(part, pltpu.HBM) for part in (cube, noise_weight)]
    far_edge, near_edge = edge_rows(sides, *stay)
    border_halo = lax.ppermute(near_edge, "sky", border)
    far_halo = lax.ppermute(far_edge, "sky", far)
    near_halo = [lax.ppermute(near_edge[i], "sky", near) for i in range(2)]
    smoothed = smooth_rows(sides, cube, noise_weight, border_halo, *near_halo)
    far_halo = pltpu.with_memory_space_constraint(far_halo, pltpu.VMEM)
    smoothed = smooth_rows(sides, cube, noise_weight, far_halo, before=smoothed)
    smoothed = lax.all_to_all(smoothed, "chan", split_axis=0, concat_axis=0, tiled=True)
    return normalize(smoothed, spectral_halo, source_mask, tile_flags, halo_width)


def solution(mesh):
    placed = (
        P("chan", "sky", None),
        P("chan", "sky", None),
        P(None, "sky", "chan"),
        P("sky", "chan"),
        P("sky", "chan"),
        P(None, "chan"),
    )
    return jax.shard_map(
        local, mesh=mesh, in_specs=placed, out_specs=P(None, None, "sky", "chan"), check_vma=False
    )
```

```python
import functools
import math

import jax
import jax.numpy as jnp
from jax import lax
from jax.experimental import pallas as pl
from jax.experimental.pallas import tpu as pltpu
from jax.sharding import PartitionSpec as P

RAD = 8
HW = 4
TILE_R = 8
TILE_C = 512
BLK = 256
LANES = 128
CHUNKS = 4
WIDTHS = (3, 5, 9)


def tap_list():
    sigma = RAD / 2.5
    return [math.exp(-((shift - RAD) ** 2) / (2.0 * sigma * sigma)) for shift in range(2 * RAD + 1)]


TAPS = tap_list()[RAD:]


def band_matrices(high_ref, low_ref):
    shape = (LANES, BLK)
    target = lax.broadcasted_iota(jnp.int32, shape, 1)
    for part, first in enumerate((0, LANES, -LANES, BLK)):
        reach = jnp.abs(lax.broadcasted_iota(jnp.int32, shape, 0) + first - target)
        band = jnp.zeros(shape, jnp.float32)
        for shift in range(RAD + 1):
            band = jnp.where(reach == shift, TAPS[shift], band)
        high = band.astype(jnp.bfloat16)
        rows = slice(part * LANES, (part + 1) * LANES)
        high_ref[rows] = high
        low_ref[rows] = (band - high.astype(jnp.float32)).astype(jnp.bfloat16)


def column_taps(tiles):
    count, width = len(tiles), tiles[0].shape[1]
    row = lax.broadcasted_iota(jnp.int32, (TILE_R, width), 0)
    totals = [
        TAPS[RAD] * (tiles[i] + tiles[i + 2]) + TAPS[0] * tiles[i + 1] for i in range(count - 2)
    ]
    for shift in range(1, TILE_R):
        rolled = [pltpu.roll(tile, TILE_R - shift, 0) for tile in tiles]
        joined = [
            jnp.where(row < TILE_R - shift, rolled[i], rolled[i + 1]) for i in range(count - 1)
        ]
        for i in range(count - 2):
            totals[i] = totals[i] + (TAPS[TILE_R - shift] * joined[i] + TAPS[shift] * joined[i + 1])
    return totals


def smooth_kernel(
    late, side_ref, cube_ref, weight_ref, *rest
):
    if late:
        halo_ref, before_ref, high_ref, low_ref, out_hbm, out_ref, sent, split, lines = rest
    else:
        halo_ref, out_ref, high_ref, low_ref, split, lines = rest
    side = side_ref[0]
    even = side == 0
    tiles_out = 1 if late else 2
    rows = tiles_out * TILE_R
    blocks = cube_ref.shape[2] // BLK
    parts = []
    top = pl.multiple_of(2 * side * TILE_R, TILE_R)
    if late:
        early = pltpu.make_async_copy(
            before_ref, out_hbm.at[:, pl.ds(pl.multiple_of((1 - side) * TILE_R, TILE_R), 2 * TILE_R)], sent.at[CHUNKS]
        )
        early.start()
        parts.append(early)
    else:
        band_matrices(high_ref, low_ref)
    split[1, :, BLK : BLK + LANES] = jnp.zeros((2 * rows, LANES), jnp.bfloat16)
    split[1, :, 3 * BLK : 3 * BLK + LANES] = jnp.zeros((2 * rows, LANES), jnp.bfloat16)
    split[blocks, :, BLK + LANES : 2 * BLK] = jnp.zeros((2 * rows, LANES), jnp.bfloat16)
    split[blocks, :, 3 * BLK + LANES :] = jnp.zeros((2 * rows, LANES), jnp.bfloat16)

    def window(ref, halo, cols):
        tile = lambda index: ref[0, pl.ds(pl.multiple_of(index * TILE_R, TILE_R), TILE_R), cols]
        if late:
            middle = tile(1)
            return [jnp.where(even, halo, middle), tile(2 * side), jnp.where(even, middle, halo)]
        return [
            jnp.where(even, tile(0), halo),
            tile(1 - side),
            tile(2 - side),
            jnp.where(even, halo, tile(2)),
        ]

    def rows_step(block, carry):
        cols = pl.ds(pl.multiple_of(block * BLK, BLK), BLK)
        cube_halo, weight_halo = halo_ref[0, :, cols], halo_ref[1, :, cols]
        weights = window(weight_ref, weight_halo, cols)
        values = window(cube_ref, cube_halo, cols)
        values = [value * weight for value, weight in zip(values, weights)]
        sides = []
        for slot, half in enumerate((0, LANES)):
            for kind, tiles in enumerate((values, weights)):
                at = 2 * slot + kind
                for i, tile in enumerate(tiles):
                    lines[at, TILE_R * i : TILE_R * (i + 1)] = tile[:, half : half + LANES]
        for slot in range(2):
            made = []
            for kind in range(2):
                at = 2 * slot + kind
                line = lambda start: lines[at, start : start + rows]
                total = TAPS[0] * line(RAD)
                for shift in range(1, RAD + 1):
                    total = total + TAPS[shift] * (line(RAD - shift) + line(RAD + shift))
                made.append(total)
            sides.append(jnp.concatenate(made, axis=0))
        both = jnp.concatenate(sides, axis=1)
        high = both.astype(jnp.bfloat16)
        low = (both - high.astype(jnp.float32)).astype(jnp.bfloat16)
        for part, base in ((high, 0), (low, 2 * BLK)):
            split[block + 1, :, base : base + BLK] = part
            split[block + 2, :, base + BLK : base + BLK + LANES] = part[:, LANES:]
            split[block, :, base + BLK + LANES : base + 2 * BLK] = part[:, :LANES]
        return carry

    lax.fori_loop(0, blocks, rows_step, 0, unroll=2)
    group = blocks // CHUNKS
    for step in range(CHUNKS):
        part = split[step * group + 1 : (step + 1) * group + 1].reshape(group * 2 * rows, 4 * BLK)
        both = jnp.dot(part[:, : 2 * BLK], high_ref[...], preferred_element_type=jnp.float32)
        both += jnp.dot(part[:, 2 * BLK :], high_ref[...], preferred_element_type=jnp.float32)
        both += jnp.dot(part[:, : 2 * BLK], low_ref[...], preferred_element_type=jnp.float32)
        both = both.reshape(group, 2 * rows, BLK)
        ratio = both[:, :rows] / both[:, rows:]
        first = step * (group // 2)
        for i in range(group):
            out_ref[first + i // 2, :, (i % 2) * BLK : (i % 2 + 1) * BLK] = ratio[i]
        if late:
            piece = pl.ds(first, group // 2)
            place = out_hbm.at[piece, pl.ds(top, rows)]
            parts.append(pltpu.make_async_copy(out_ref.at[piece], place, sent.at[step]))
            parts[-1].start()
    for copy in parts:
        copy.wait()


def edge_kernel(side_ref, cube_ref, weight_ref, far_ref, near_ref, done):
    side = side_ref[0]
    columns = cube_ref.shape[2]
    last = cube_ref.shape[1] - TILE_R
    copies = []
    for k, (out_ref, start) in enumerate(((far_ref, side * last), (near_ref, (1 - side) * last))):
        rows = pl.ds(pl.multiple_of(start, TILE_R), TILE_R)
        for j, ref in enumerate((cube_ref, weight_ref)):
            place = out_ref.at[j, :, :columns]
            copies.append(pltpu.make_async_copy(ref.at[0, rows], place, done.at[2 * k + j]))
    for copy in copies:
        copy.start()
    far_ref[:, :, columns:] = jnp.zeros((2, TILE_R, LANES), jnp.float32)
    for copy in copies:
        copy.wait()


def edge_rows(side, cube, weight):
    columns = cube.shape[2]
    edges = [pltpu.VMEM((2, TILE_R, columns + extra), cube.dtype) for extra in (LANES, 0)]
    whole = pl.BlockSpec(memory_space=pltpu.VMEM)
    return pl.pallas_call(
        edge_kernel,
        out_shape=edges,
        in_specs=[pl.BlockSpec(memory_space=pltpu.SMEM)] + [pl.BlockSpec(memory_space=pl.ANY)] * 2,
        out_specs=[whole] * 2,
        scratch_shapes=[pltpu.SemaphoreType.DMA((4,))],
        compiler_params=pltpu.CompilerParams(vmem_limit_bytes=8 * 1024 * 1024),
        cost_estimate=pl.CostEstimate(
            flops=10**11, bytes_accessed=64 * TILE_R * columns, transcendentals=0
        ),
    )(side, cube, weight)


def smooth_rows(side, cube, weight, halo, before=()):
    late = len(before) > 0
    rows = TILE_R if late else 2 * TILE_R
    columns = cube.shape[2]
    tiles = columns // TILE_C
    blocks = columns // BLK
    whole = pl.BlockSpec(memory_space=pltpu.VMEM)
    part = pltpu.VMEM((tiles, rows, TILE_C), jnp.float32)
    band = pltpu.VMEM((2 * BLK, BLK), jnp.bfloat16)
    scratch = [
        pltpu.VMEM((blocks + 2, 2 * rows, 4 * BLK), jnp.bfloat16),
        pltpu.VMEM((4, rows + 2 * TILE_R, LANES), jnp.float32),
    ]
    if late:
        scratch = [part, pltpu.SemaphoreType.DMA((CHUNKS + 1,))] + scratch
    return pl.pallas_call(
        functools.partial(smooth_kernel, late),
        out_shape=pltpu.HBM((tiles, cube.shape[1], TILE_C), jnp.float32) if late else [part, band, band],
        in_specs=[pl.BlockSpec(memory_space=pltpu.SMEM)] + [whole] * (3 + len(before)),
        out_specs=pl.BlockSpec(memory_space=pl.ANY) if late else [whole] * 3,
        scratch_shapes=scratch,
        compiler_params=pltpu.CompilerParams(vmem_limit_bytes=24 * 1024 * 1024),
        cost_estimate=pl.CostEstimate(flops=0, bytes_accessed=0, transcendentals=0),
    )(side, cube, weight, halo, *before)


def norm_kernel(smooth_ref, halo_ref, mask_ref, flags_ref, width_ref, out_hbm, out_ref, sent):
    channels, rows, columns = smooth_ref.shape
    keep_low = [(j >= HW - width_ref[0, 0]).astype(jnp.float32) for j in range(HW)]
    keep_high = [(j < width_ref[1, 0]).astype(jnp.float32) for j in range(HW)]

    def whole(x):
        return jnp.sum(jnp.sum(x, axis=1, keepdims=True), axis=0, keepdims=True)

    copies = []
    for tile in range(rows // TILE_R):
        lines = slice(tile * TILE_R, (tile + 1) * TILE_R)
        sums = [jnp.zeros((TILE_R, LANES), jnp.float32) for _ in WIDTHS]
        kept = jnp.zeros((TILE_R, LANES), jnp.float32)
        for strip in range(columns // LANES):
            cols = slice(strip * LANES, (strip + 1) * LANES)
            keep = (mask_ref[lines, cols] == 0).astype(jnp.float32)
            kept = kept + keep
            extended = [halo_ref[j, lines, cols] * keep_low[j] for j in range(HW)]
            extended += [smooth_ref[c, lines, cols] for c in range(channels)]
            extended += [halo_ref[HW + j, lines, cols] * keep_high[j] for j in range(HW)]
            squares = [jnp.zeros((TILE_R, LANES), jnp.float32) for _ in WIDTHS]
            for c in range(channels):
                at = c + HW
                total = extended[at]
                reach = 0
                for i, width in enumerate(WIDTHS):
                    while reach < width // 2:
                        reach += 1
                        total = total + (extended[at - reach] + extended[at + reach])
                    out_ref[i, c, lines, cols] = total
                    squares[i] = squares[i] + total * total
            sums = [total + square * keep for total, square in zip(sums, squares)]
        count = jnp.maximum(whole(kept) * channels, 1.0)
        flag = flags_ref[tile, 0].astype(jnp.float32)
        for i, width in enumerate(WIDTHS):
            factor = flag / (jnp.sqrt(whole(sums[i]) / (count * width**2) + 1e-06) * width)
            factor = jnp.broadcast_to(factor, (TILE_R, columns))
            for c in range(channels):
                out_ref[i, c, lines] = out_ref[i, c, lines] * factor
            copies.append(
                pltpu.make_async_copy(out_ref.at[i, :, lines], out_hbm.at[i, :, lines], sent.at[tile, i])
            )
            copies[-1].start()
    for copy in copies:
        copy.wait()


def normalize(smoothed, halo, mask, flags, widths):
    out = (len(WIDTHS),) + smoothed.shape
    whole = pl.BlockSpec(memory_space=pltpu.VMEM)
    scalars = pl.BlockSpec(memory_space=pltpu.SMEM)
    return pl.pallas_call(
        norm_kernel,
        out_shape=jax.ShapeDtypeStruct(out, jnp.float32),
        in_specs=[whole, whole, whole, scalars, scalars],
        out_specs=pl.BlockSpec(memory_space=pl.ANY),
        scratch_shapes=[
            pltpu.VMEM(out, jnp.float32),
            pltpu.SemaphoreType.DMA((smoothed.shape[1] // TILE_R, len(WIDTHS))),
        ],
        compiler_params=pltpu.CompilerParams(vmem_limit_bytes=16 * 1024 * 1024),
        cost_estimate=pl.CostEstimate(
            flops=30 * smoothed.size, bytes_accessed=20 * smoothed.size, transcendentals=0
        ),
    )(smoothed, halo, mask, flags, widths)


def local(cube, noise_weight, spectral_halo, source_mask, tile_flags, halo_width):
    sky = lax.axis_size("sky")
    side = lax.axis_index("sky") & 1
    near = [(i, i ^ 1) for i in range(sky)]
    far = [(i, i + 1) for i in range(1, sky - 1, 2)]
    far = far + [(target, source) for source, target in far]
    sides = jnp.reshape(side, (1,))
    stay = [pltpu.with_memory_space_constraint(part, pltpu.HBM) for part in (cube, noise_weight)]
    far_edge, near_edge = edge_rows(sides, *stay)
    far_halo = lax.ppermute(far_edge, "sky", far)
    near_halo = lax.ppermute(near_edge, "sky", near)
    smoothed = smooth_rows(sides, cube, noise_weight, near_halo)
    far_halo = pltpu.with_memory_space_constraint(far_halo, pltpu.VMEM)
    smoothed = smooth_rows(sides, cube, noise_weight, far_halo, before=smoothed)
    smoothed = lax.all_to_all(smoothed, "chan", split_axis=0, concat_axis=0, tiled=True)
    return normalize(smoothed, spectral_halo, source_mask, tile_flags, halo_width)


def solution(mesh):
    placed = (
        P("chan", "sky", None),
        P("chan", "sky", None),
        P(None, "sky", "chan"),
        P("sky", "chan"),
        P("sky", "chan"),
        P(None, "chan"),
    )
    return jax.shard_map(
        local, mesh=mesh, in_specs=placed, out_specs=P(None, None, "sky", "chan"), check_vma=False
    )
```

```python
import functools
import math

import jax
import jax.numpy as jnp
from jax import lax
from jax.experimental import pallas as pl
from jax.experimental.pallas import tpu as pltpu
from jax.sharding import PartitionSpec as P

RAD = 8
HW = 4
TILE_R = 8
TILE_C = 512
BLK = 256
LANES = 128
CHUNKS = 4
UNROLL = 4
WIDTHS = (3, 5, 9)


def tap_list():
    sigma = RAD / 2.5
    return [math.exp(-((shift - RAD) ** 2) / (2.0 * sigma * sigma)) for shift in range(2 * RAD + 1)]


TAPS = tap_list()[RAD:]


def band_matrices(high_ref, low_ref):
    shape = (LANES, BLK)
    target = lax.broadcasted_iota(jnp.int32, shape, 1)
    for part, first in enumerate((0, LANES, -LANES, BLK)):
        reach = jnp.abs(lax.broadcasted_iota(jnp.int32, shape, 0) + first - target)
        band = jnp.zeros(shape, jnp.float32)
        for shift in range(RAD + 1):
            band = jnp.where(reach == shift, TAPS[shift], band)
        high = band.astype(jnp.bfloat16)
        rows = slice(part * LANES, (part + 1) * LANES)
        high_ref[rows] = high
        low_ref[rows] = (band - high.astype(jnp.float32)).astype(jnp.bfloat16)


def smooth_kernel(kind, side_ref, cube_ref, weight_ref, *rest):
    if kind == "middle":
        out_ref, high_ref, low_ref, split, lines = rest
    elif kind == "near":
        halo_ref, high_ref, low_ref, out_ref, split, lines = rest
    else:
        halo_ref, high_ref, low_ref, middle_ref, near_ref, out_hbm, out_ref, sent, split, lines = rest
    side = 1 - side_ref[0] if kind == "near" else side_ref[0]
    top = side == 0
    blocks = cube_ref.shape[2] // BLK
    copies = []
    if kind == "far":
        for slot, (ref, tile) in enumerate(((middle_ref, 1), (near_ref, 2 * (1 - side)))):
            place = out_hbm.at[:, pl.ds(pl.multiple_of(tile * TILE_R, TILE_R), TILE_R)]
            copies.append(pltpu.make_async_copy(ref, place, sent.at[CHUNKS + slot]))
            copies[-1].start()
    if kind == "middle":
        band_matrices(high_ref, low_ref)
    edge = jnp.zeros((2 * TILE_R, LANES), jnp.bfloat16)
    for first in (BLK, 3 * BLK):
        split[1, :, first : first + LANES] = edge
        split[blocks, :, first + LANES : first + BLK] = edge

    def window(ref, halo, cols):
        tile = lambda index: ref[0, pl.ds(pl.multiple_of(index * TILE_R, TILE_R), TILE_R), cols]
        if kind == "middle":
            return [tile(0), tile(1), tile(2)]
        centre = tile(1)
        return [jnp.where(top, halo, centre), tile(2 * side), jnp.where(top, centre, halo)]

    def rows_step(block, carry):
        cols = pl.ds(pl.multiple_of(block * BLK, BLK), BLK)
        halo = [None, None] if kind == "middle" else [halo_ref[0, :, cols], halo_ref[1, :, cols]]
        weights = window(weight_ref, halo[1], cols)
        values = [value * weight for value, weight in zip(window(cube_ref, halo[0], cols), weights)]
        for half in range(2):
            for at, tiles in ((2 * half, values), (2 * half + 1, weights)):
                for i, tile in enumerate(tiles):
                    lines[at, TILE_R * i : TILE_R * (i + 1)] = tile[:, half * LANES : (half + 1) * LANES]
        halves = []
        for half in range(2):
            made = []
            for at in (2 * half, 2 * half + 1):
                line = lambda start: lines[at, start : start + TILE_R]
                total = TAPS[0] * line(RAD)
                for shift in range(1, RAD + 1):
                    total = total + TAPS[shift] * (line(RAD - shift) + line(RAD + shift))
                made.append(total)
            halves.append(jnp.concatenate(made, axis=0))
        both = jnp.concatenate(halves, axis=1)
        high = both.astype(jnp.bfloat16)
        low = (both - high.astype(jnp.float32)).astype(jnp.bfloat16)
        for part, base in ((high, 0), (low, 2 * BLK)):
            split[block + 1, :, base : base + BLK] = part
            split[block + 2, :, base + BLK : base + BLK + LANES] = part[:, LANES:]
            split[block, :, base + BLK + LANES : base + 2 * BLK] = part[:, :LANES]
        return carry

    lax.fori_loop(0, blocks, rows_step, 0, unroll=UNROLL)

    group = blocks // CHUNKS
    for step in range(CHUNKS):
        part = split[step * group + 1 : (step + 1) * group + 1].reshape(group * 2 * TILE_R, 4 * BLK)
        both = jnp.dot(part[:, : 2 * BLK], high_ref[...], preferred_element_type=jnp.float32)
        both += jnp.dot(part[:, 2 * BLK :], high_ref[...], preferred_element_type=jnp.float32)
        both += jnp.dot(part[:, : 2 * BLK], low_ref[...], preferred_element_type=jnp.float32)
        both = both.reshape(group, 2 * TILE_R, BLK)
        ratio = both[:, :TILE_R] / both[:, TILE_R:]
        first = step * (group // 2)
        for i in range(group):
            out_ref[first + i // 2, :, (i % 2) * BLK : (i % 2 + 1) * BLK] = ratio[i]
        if kind == "far":
            piece = pl.ds(first, group // 2)
            place = out_hbm.at[piece, pl.ds(pl.multiple_of(2 * side * TILE_R, TILE_R), TILE_R)]
            copies.append(pltpu.make_async_copy(out_ref.at[piece], place, sent.at[step]))
            copies[-1].start()
    for copy in copies:
        copy.wait()


def edge_kernel(side_ref, cube_ref, weight_ref, far_ref, near_ref, done):
    side = side_ref[0]
    columns = cube_ref.shape[2]
    last = cube_ref.shape[1] - TILE_R
    copies = []
    for k, (out_ref, start) in enumerate(((far_ref, side * last), (near_ref, (1 - side) * last))):
        rows = pl.ds(pl.multiple_of(start, TILE_R), TILE_R)
        for j, ref in enumerate((cube_ref, weight_ref)):
            place = out_ref.at[j, :, :columns]
            copies.append(pltpu.make_async_copy(ref.at[0, rows], place, done.at[2 * k + j]))
    for copy in copies:
        copy.start()
    far_ref[:, :, columns:] = jnp.zeros((2, TILE_R, LANES), jnp.float32)
    for copy in copies:
        copy.wait()


def edge_rows(side, cube, weight):
    columns = cube.shape[2]
    edges = [pltpu.VMEM((2, TILE_R, columns + extra), cube.dtype) for extra in (LANES, 0)]
    whole = pl.BlockSpec(memory_space=pltpu.VMEM)
    return pl.pallas_call(
        edge_kernel,
        out_shape=edges,
        in_specs=[pl.BlockSpec(memory_space=pltpu.SMEM)] + [pl.BlockSpec(memory_space=pl.ANY)] * 2,
        out_specs=[whole] * 2,
        scratch_shapes=[pltpu.SemaphoreType.DMA((4,))],
        compiler_params=pltpu.CompilerParams(vmem_limit_bytes=8 * 1024 * 1024),
        cost_estimate=pl.CostEstimate(
            flops=10**11, bytes_accessed=64 * TILE_R * columns, transcendentals=0
        ),
    )(side, cube, weight)


def smooth_rows(kind, side, cube, weight, *rest):
    columns = cube.shape[2]
    tiles = columns // TILE_C
    whole = pl.BlockSpec(memory_space=pltpu.VMEM)
    part = pltpu.VMEM((tiles, TILE_R, TILE_C), jnp.float32)
    band = pltpu.VMEM((2 * BLK, BLK), jnp.bfloat16)
    out_shape, out_specs, scratch = part, whole, []
    if kind == "middle":
        out_shape, out_specs = [part, band, band], [whole] * 3
    if kind == "far":
        out_shape = pltpu.HBM((tiles, cube.shape[1], TILE_C), jnp.float32)
        out_specs = pl.BlockSpec(memory_space=pl.ANY)
        scratch = [part, pltpu.SemaphoreType.DMA((CHUNKS + 2,))]
    return pl.pallas_call(
        functools.partial(smooth_kernel, kind),
        out_shape=out_shape,
        in_specs=[pl.BlockSpec(memory_space=pltpu.SMEM)] + [whole] * (2 + len(rest)),
        out_specs=out_specs,
        scratch_shapes=scratch
        + [
            pltpu.VMEM((columns // BLK + 2, 2 * TILE_R, 4 * BLK), jnp.bfloat16),
            pltpu.VMEM((4, 3 * TILE_R, LANES), jnp.float32),
        ],
        compiler_params=pltpu.CompilerParams(vmem_limit_bytes=24 * 1024 * 1024),
        cost_estimate=pl.CostEstimate(flops=0, bytes_accessed=0, transcendentals=0),
    )(side, cube, weight, *rest)


def norm_kernel(smooth_ref, halo_ref, mask_ref, flags_ref, width_ref, out_hbm, out_ref, sent):
    channels, rows, columns = smooth_ref.shape
    shape = (TILE_R, LANES)
    below = jnp.broadcast_to(width_ref[0:1, :], shape)
    above = jnp.broadcast_to(width_ref[1:2, :], shape)
    keep_low = [(below >= HW - j).astype(jnp.float32) for j in range(HW)]
    keep_high = [(above > j).astype(jnp.float32) for j in range(HW)]

    def whole(x):
        return jnp.sum(jnp.sum(x, axis=1, keepdims=True), axis=0, keepdims=True)

    copies = []
    for tile in range(rows // TILE_R):
        lines = slice(tile * TILE_R, (tile + 1) * TILE_R)
        sums = [jnp.zeros((TILE_R, LANES), jnp.float32) for _ in WIDTHS]
        kept = jnp.zeros((TILE_R, LANES), jnp.float32)
        for strip in range(columns // LANES):
            cols = slice(strip * LANES, (strip + 1) * LANES)
            keep = (mask_ref[lines, cols] == 0).astype(jnp.float32)
            kept = kept + keep
            extended = [halo_ref[j, lines, cols] * keep_low[j] for j in range(HW)]
            extended += [smooth_ref[c, lines, cols] for c in range(channels)]
            extended += [halo_ref[HW + j, lines, cols] * keep_high[j] for j in range(HW)]
            squares = [jnp.zeros((TILE_R, LANES), jnp.float32) for _ in WIDTHS]
            for c in range(channels):
                at = c + HW
                total = extended[at]
                reach = 0
                for i, width in enumerate(WIDTHS):
                    while reach < width // 2:
                        reach += 1
                        total = total + (extended[at - reach] + extended[at + reach])
                    out_ref[i, c, lines, cols] = total
                    squares[i] = squares[i] + total * total
            sums = [total + square * keep for total, square in zip(sums, squares)]
        count = jnp.maximum(whole(kept) * channels, 1.0)
        flag = flags_ref[tile : tile + 1, :].astype(jnp.float32)
        for i, width in enumerate(WIDTHS):
            factor = flag / (jnp.sqrt(whole(sums[i]) / (count * width**2) + 1e-06) * width)
            factor = jnp.broadcast_to(factor, (TILE_R, columns))
            for c in range(channels):
                out_ref[i, c, lines] = out_ref[i, c, lines] * factor
            copies.append(
                pltpu.make_async_copy(out_ref.at[i, :, lines], out_hbm.at[i, :, lines], sent.at[tile, i])
            )
            copies[-1].start()
    for copy in copies:
        copy.wait()


def normalize(smoothed, halo, mask, flags, widths):
    out = (len(WIDTHS),) + smoothed.shape
    whole = pl.BlockSpec(memory_space=pltpu.VMEM)
    return pl.pallas_call(
        norm_kernel,
        out_shape=jax.ShapeDtypeStruct(out, jnp.float32),
        in_specs=[whole] * 5,
        out_specs=pl.BlockSpec(memory_space=pl.ANY),
        scratch_shapes=[
            pltpu.VMEM(out, jnp.float32),
            pltpu.SemaphoreType.DMA((smoothed.shape[1] // TILE_R, len(WIDTHS))),
        ],
        compiler_params=pltpu.CompilerParams(vmem_limit_bytes=16 * 1024 * 1024),
        cost_estimate=pl.CostEstimate(
            flops=30 * smoothed.size, bytes_accessed=20 * smoothed.size, transcendentals=0
        ),
    )(smoothed, halo, mask, flags, widths)


def local(cube, noise_weight, spectral_halo, source_mask, tile_flags, halo_width):
    sky = lax.axis_size("sky")
    side = lax.axis_index("sky") & 1
    near = [(i, i ^ 1) for i in range(sky)]
    far = [(i, i + 1) for i in range(1, sky - 1, 2)]
    far = far + [(target, source) for source, target in far]
    sides = jnp.reshape(side, (1,))
    stay = [pltpu.with_memory_space_constraint(part, pltpu.HBM) for part in (cube, noise_weight)]
    far_edge, near_edge = edge_rows(sides, *stay)
    far_halo = lax.ppermute(far_edge, "sky", far)
    near_halo = lax.ppermute(near_edge, "sky", near)
    middle, *band = smooth_rows("middle", sides, cube, noise_weight)
    near_part = smooth_rows("near", sides, cube, noise_weight, near_halo, *band)
    far_halo = pltpu.with_memory_space_constraint(far_halo, pltpu.VMEM)
    smoothed = smooth_rows("far", sides, cube, noise_weight, far_halo, *band, middle, near_part)
    smoothed = lax.all_to_all(smoothed, "chan", split_axis=0, concat_axis=0, tiled=True)
    return normalize(smoothed, spectral_halo, source_mask, tile_flags, halo_width)


def solution(mesh):
    placed = (
        P("chan", "sky", None),
        P("chan", "sky", None),
        P(None, "sky", "chan"),
        P("sky", "chan"),
        P("sky", "chan"),
        P(None, "chan"),
    )
    return jax.shard_map(
        local, mesh=mesh, in_specs=placed, out_specs=P(None, None, "sky", "chan"), check_vma=False
    )
```

```python
import functools
import math

import jax
import jax.numpy as jnp
from jax import lax
from jax.experimental import pallas as pl
from jax.experimental.pallas import tpu as pltpu
from jax.sharding import PartitionSpec as P

RAD = 8
HW = 4
TILE_R = 8
TILE_C = 512
BLK = 256
LANES = 128
CHUNKS = 4
UNROLL = 4
SHARE = 2.0**-7
WIDTHS = (3, 5, 9)


def tap_list():
    sigma = RAD / 2.5
    return [math.exp(-((shift - RAD) ** 2) / (2.0 * sigma * sigma)) for shift in range(2 * RAD + 1)]


TAPS = tap_list()[RAD:]


def band_matrices(high_ref, low_ref):
    shape = (LANES, BLK)
    target = lax.broadcasted_iota(jnp.int32, shape, 1)
    for part, first in enumerate((0, LANES, -LANES, BLK)):
        reach = jnp.abs(lax.broadcasted_iota(jnp.int32, shape, 0) + first - target)
        band = jnp.zeros(shape, jnp.float32)
        for shift in range(RAD + 1):
            band = jnp.where(reach == shift, TAPS[shift], band)
        high = band.astype(jnp.bfloat16)
        rows = slice(part * LANES, (part + 1) * LANES)
        high_ref[rows] = high
        low_ref[rows] = (band - high.astype(jnp.float32)).astype(jnp.bfloat16)


def smooth_kernel(kind, side_ref, cube_ref, weight_ref, *rest):
    if kind == "middle":
        out_ref, high_ref, low_ref, split, lines = rest
    elif kind == "near":
        halo_ref, high_ref, low_ref, out_ref, split, lines = rest
    else:
        halo_ref, high_ref, low_ref, middle_ref, near_ref, out_hbm, out_ref, sent, split, lines = rest
    side = 1 - side_ref[0] if kind == "near" else side_ref[0]
    top = side == 0
    blocks = cube_ref.shape[2] // BLK
    copies = []
    if kind == "far":
        for slot, (ref, tile) in enumerate(((middle_ref, 1), (near_ref, 2 * (1 - side)))):
            place = out_hbm.at[:, pl.ds(pl.multiple_of(tile * TILE_R, TILE_R), TILE_R)]
            copies.append(pltpu.make_async_copy(ref, place, sent.at[CHUNKS + slot]))
            copies[-1].start()
    if kind == "middle":
        band_matrices(high_ref, low_ref)
    edge = jnp.zeros((2 * TILE_R, LANES), jnp.bfloat16)
    for first in (BLK, 3 * BLK):
        split[1, :, first : first + LANES] = edge
        split[blocks, :, first + LANES : first + BLK] = edge

    def window(ref, halo, cols):
        tile = lambda index: ref[0, pl.ds(pl.multiple_of(index * TILE_R, TILE_R), TILE_R), cols]
        if kind == "middle":
            return [tile(0), tile(1), tile(2)]
        centre = tile(1)
        return [jnp.where(top, halo, centre), tile(2 * side), jnp.where(top, centre, halo)]

    def rows_step(block, carry):
        cols = pl.ds(pl.multiple_of(block * BLK, BLK), BLK)
        halo = [None, None] if kind == "middle" else [halo_ref[0, :, cols], halo_ref[1, :, cols]]
        weights = [tile * SHARE for tile in window(weight_ref, halo[1], cols)]
        values = [value * weight for value, weight in zip(window(cube_ref, halo[0], cols), weights)]
        for half in range(2):
            for at, tiles in ((2 * half, values), (2 * half + 1, weights)):
                for i, tile in enumerate(tiles):
                    lines[at, TILE_R * i : TILE_R * (i + 1)] = tile[:, half * LANES : (half + 1) * LANES]
        halves = []
        for half in range(2):
            made = []
            for at in (2 * half, 2 * half + 1):
                line = lambda start: lines[at, start : start + TILE_R]
                total = TAPS[0] * line(RAD)
                for shift in range(1, RAD + 1):
                    total = total + TAPS[shift] * (line(RAD - shift) + line(RAD + shift))
                made.append(total)
            halves.append(jnp.concatenate(made, axis=0))
        both = jnp.concatenate(halves, axis=1)
        high = both.astype(jnp.bfloat16)
        low = (both - high.astype(jnp.float32)).astype(jnp.bfloat16)
        for part, base in ((high, 0), (low, 2 * BLK)):
            split[block + 1, :, base : base + BLK] = part
            split[block + 2, :, base + BLK : base + BLK + LANES] = part[:, LANES:]
            split[block, :, base + BLK + LANES : base + 2 * BLK] = part[:, :LANES]
        return carry

    lax.fori_loop(0, blocks, rows_step, 0, unroll=UNROLL)

    group = blocks // CHUNKS
    for step in range(CHUNKS):
        part = split[step * group + 1 : (step + 1) * group + 1].reshape(group * 2 * TILE_R, 4 * BLK)
        both = jnp.dot(part[:, : 2 * BLK], high_ref[...], preferred_element_type=jnp.float32)
        both += jnp.dot(part[:, 2 * BLK :], high_ref[...], preferred_element_type=jnp.float32)
        both += jnp.dot(part[:, : 2 * BLK], low_ref[...], preferred_element_type=jnp.float32)
        both = both.reshape(group, 2 * TILE_R, BLK)
        ratio = both[:, :TILE_R] / both[:, TILE_R:]
        first = step * (group // 2)
        for i in range(group):
            out_ref[first + i // 2, :, (i % 2) * BLK : (i % 2 + 1) * BLK] = ratio[i]
        if kind == "far":
            piece = pl.ds(first, group // 2)
            place = out_hbm.at[piece, pl.ds(pl.multiple_of(2 * side * TILE_R, TILE_R), TILE_R)]
            copies.append(pltpu.make_async_copy(out_ref.at[piece], place, sent.at[step]))
            copies[-1].start()
    for copy in copies:
        copy.wait()


def edge_kernel(side_ref, cube_ref, weight_ref, far_ref, near_ref, done):
    side = side_ref[0]
    columns = cube_ref.shape[2]
    last = cube_ref.shape[1] - TILE_R
    copies = []
    for k, (out_ref, start) in enumerate(((far_ref, side * last), (near_ref, (1 - side) * last))):
        rows = pl.ds(pl.multiple_of(start, TILE_R), TILE_R)
        for j, ref in enumerate((cube_ref, weight_ref)):
            place = out_ref.at[j, :, :columns]
            copies.append(pltpu.make_async_copy(ref.at[0, rows], place, done.at[2 * k + j]))
    for copy in copies:
        copy.start()
    far_ref[:, :, columns:] = jnp.zeros((2, TILE_R, LANES), jnp.float32)
    for copy in copies:
        copy.wait()


def edge_rows(side, cube, weight):
    columns = cube.shape[2]
    edges = [pltpu.VMEM((2, TILE_R, columns + extra), cube.dtype) for extra in (LANES, 0)]
    whole = pl.BlockSpec(memory_space=pltpu.VMEM)
    return pl.pallas_call(
        edge_kernel,
        out_shape=edges,
        in_specs=[pl.BlockSpec(memory_space=pltpu.SMEM)] + [pl.BlockSpec(memory_space=pl.ANY)] * 2,
        out_specs=[whole] * 2,
        scratch_shapes=[pltpu.SemaphoreType.DMA((4,))],
        compiler_params=pltpu.CompilerParams(vmem_limit_bytes=8 * 1024 * 1024),
        cost_estimate=pl.CostEstimate(
            flops=10**11, bytes_accessed=64 * TILE_R * columns, transcendentals=0
        ),
    )(side, cube, weight)


def smooth_rows(kind, side, cube, weight, *rest):
    columns = cube.shape[2]
    tiles = columns // TILE_C
    whole = pl.BlockSpec(memory_space=pltpu.VMEM)
    part = pltpu.VMEM((tiles, TILE_R, TILE_C), jnp.float32)
    band = pltpu.VMEM((2 * BLK, BLK), jnp.bfloat16)
    out_shape, out_specs, scratch = part, whole, []
    if kind == "middle":
        out_shape, out_specs = [part, band, band], [whole] * 3
    if kind == "far":
        out_shape = pltpu.HBM((tiles, cube.shape[1], TILE_C), jnp.float32)
        out_specs = pl.BlockSpec(memory_space=pl.ANY)
        scratch = [part, pltpu.SemaphoreType.DMA((CHUNKS + 2,))]
    return pl.pallas_call(
        functools.partial(smooth_kernel, kind),
        out_shape=out_shape,
        in_specs=[pl.BlockSpec(memory_space=pltpu.SMEM)] + [whole] * (2 + len(rest)),
        out_specs=out_specs,
        scratch_shapes=scratch
        + [
            pltpu.VMEM((columns // BLK + 2, 2 * TILE_R, 4 * BLK), jnp.bfloat16),
            pltpu.VMEM((4, 3 * TILE_R, LANES), jnp.float32),
        ],
        compiler_params=pltpu.CompilerParams(vmem_limit_bytes=24 * 1024 * 1024),
        cost_estimate=pl.CostEstimate(flops=0, bytes_accessed=0, transcendentals=0),
    )(side, cube, weight, *rest)


def norm_kernel(smooth_ref, halo_ref, mask_ref, flags_ref, width_ref, out_hbm, out_ref, sent):
    channels, rows, columns = smooth_ref.shape
    shape = (TILE_R, LANES)
    below = jnp.broadcast_to(width_ref[0:1, :], shape)
    above = jnp.broadcast_to(width_ref[1:2, :], shape)
    keep_low = [(below >= HW - j).astype(jnp.float32) for j in range(HW)]
    keep_high = [(above > j).astype(jnp.float32) for j in range(HW)]

    def whole(x):
        return jnp.sum(jnp.sum(x, axis=1, keepdims=True), axis=0, keepdims=True)

    copies = []
    for tile in range(rows // TILE_R):
        lines = slice(tile * TILE_R, (tile + 1) * TILE_R)
        sums = [jnp.zeros((TILE_R, LANES), jnp.float32) for _ in WIDTHS]
        kept = jnp.zeros((TILE_R, LANES), jnp.float32)
        for strip in range(columns // LANES):
            cols = slice(strip * LANES, (strip + 1) * LANES)
            keep = (mask_ref[lines, cols] == 0).astype(jnp.float32)
            kept = kept + keep
            extended = [halo_ref[j, lines, cols] * keep_low[j] for j in range(HW)]
            extended += [smooth_ref[c, lines, cols] for c in range(channels)]
            extended += [halo_ref[HW + j, lines, cols] * keep_high[j] for j in range(HW)]
            squares = [jnp.zeros((TILE_R, LANES), jnp.float32) for _ in WIDTHS]
            for c in range(channels):
                at = c + HW
                total = extended[at]
                reach = 0
                for i, width in enumerate(WIDTHS):
                    while reach < width // 2:
                        reach += 1
                        total = total + (extended[at - reach] + extended[at + reach])
                    boxcar = total * (1.0 / width)
                    out_ref[i, c, lines, cols] = boxcar
                    squares[i] = squares[i] + boxcar * boxcar
            sums = [total + square * keep for total, square in zip(sums, squares)]
        count = jnp.maximum(whole(kept) * channels, 1.0)
        flag = flags_ref[tile : tile + 1, :].astype(jnp.float32)
        for i in range(len(WIDTHS)):
            factor = flag / jnp.sqrt(whole(sums[i]) / count + 1e-06)
            factor = jnp.broadcast_to(factor, (TILE_R, columns))
            for c in range(channels):
                out_ref[i, c, lines] = out_ref[i, c, lines] * factor
            copies.append(
                pltpu.make_async_copy(out_ref.at[i, :, lines], out_hbm.at[i, :, lines], sent.at[tile, i])
            )
            copies[-1].start()
    for copy in copies:
        copy.wait()


def normalize(smoothed, halo, mask, flags, widths):
    out = (len(WIDTHS),) + smoothed.shape
    whole = pl.BlockSpec(memory_space=pltpu.VMEM)
    return pl.pallas_call(
        norm_kernel,
        out_shape=jax.ShapeDtypeStruct(out, jnp.float32),
        in_specs=[whole] * 5,
        out_specs=pl.BlockSpec(memory_space=pl.ANY),
        scratch_shapes=[
            pltpu.VMEM(out, jnp.float32),
            pltpu.SemaphoreType.DMA((smoothed.shape[1] // TILE_R, len(WIDTHS))),
        ],
        compiler_params=pltpu.CompilerParams(vmem_limit_bytes=16 * 1024 * 1024),
        cost_estimate=pl.CostEstimate(
            flops=30 * smoothed.size, bytes_accessed=20 * smoothed.size, transcendentals=0
        ),
    )(smoothed, halo, mask, flags, widths)


def local(cube, noise_weight, spectral_halo, source_mask, tile_flags, halo_width):
    sky = lax.axis_size("sky")
    side = lax.axis_index("sky") & 1
    near = [(i, i ^ 1) for i in range(sky)]
    far = [(i, i + 1) for i in range(1, sky - 1, 2)]
    far = far + [(target, source) for source, target in far]
    sides = jnp.reshape(side, (1,))
    stay = [pltpu.with_memory_space_constraint(part, pltpu.HBM) for part in (cube, noise_weight)]
    far_edge, near_edge = edge_rows(sides, *stay)
    far_halo = lax.ppermute(far_edge, "sky", far)
    near_halo = lax.ppermute(near_edge, "sky", near)
    middle, *band = smooth_rows("middle", sides, cube, noise_weight)
    near_part = smooth_rows("near", sides, cube, noise_weight, near_halo, *band)
    far_halo = pltpu.with_memory_space_constraint(far_halo, pltpu.VMEM)
    smoothed = smooth_rows("far", sides, cube, noise_weight, far_halo, *band, middle, near_part)
    smoothed = lax.all_to_all(smoothed, "chan", split_axis=0, concat_axis=0, tiled=True)
    return normalize(smoothed, spectral_halo, source_mask, tile_flags, halo_width)


def solution(mesh):
    placed = (
        P("chan", "sky", None),
        P("chan", "sky", None),
        P(None, "sky", "chan"),
        P("sky", "chan"),
        P("sky", "chan"),
        P(None, "chan"),
    )
    return jax.shard_map(
        local, mesh=mesh, in_specs=placed, out_specs=P(None, None, "sky", "chan"), check_vma=False
    )
```

```python
import functools
import math

import jax
import jax.numpy as jnp
from jax import lax
from jax.experimental import pallas as pl
from jax.experimental.pallas import tpu as pltpu
from jax.sharding import PartitionSpec as P

RAD = 8
HW = 4
TILE_R = 8
TILE_C = 512
BLK = 256
LANES = 128
CHUNKS = 4
UNROLL = 4
SHARE = 2.0**-7
WIDTHS = (3, 5, 9)


def tap_list():
    sigma = RAD / 2.5
    return [math.exp(-((shift - RAD) ** 2) / (2.0 * sigma * sigma)) for shift in range(2 * RAD + 1)]


TAPS = tap_list()[RAD:]


def band_matrices(high_ref, low_ref):
    shape = (LANES, BLK)
    target = lax.broadcasted_iota(jnp.int32, shape, 1)
    for part, first in enumerate((0, LANES, -LANES, BLK)):
        reach = jnp.abs(lax.broadcasted_iota(jnp.int32, shape, 0) + first - target)
        band = jnp.zeros(shape, jnp.float32)
        for shift in range(RAD + 1):
            band = jnp.where(reach == shift, TAPS[shift], band)
        high = band.astype(jnp.bfloat16)
        rows = slice(part * LANES, (part + 1) * LANES)
        high_ref[rows] = high
        low_ref[rows] = (band - high.astype(jnp.float32)).astype(jnp.bfloat16)


def smooth_kernel(kind, side_ref, cube_ref, weight_ref, *rest):
    if kind == "middle":
        high_ref, low_ref, out_ref, split, lines = rest
    elif kind == "near":
        halo_ref, high_ref, low_ref, out_ref, split, lines = rest
    else:
        halo_ref, high_ref, low_ref, middle_ref, near_ref, out_hbm, out_ref, sent, split, lines = rest
    side = 1 - side_ref[0] if kind == "near" else side_ref[0]
    top = side == 0
    blocks = cube_ref.shape[2] // BLK
    copies = []
    if kind == "far":
        for slot, (ref, tile) in enumerate(((middle_ref, 1), (near_ref, 2 * (1 - side)))):
            place = out_hbm.at[:, pl.ds(pl.multiple_of(tile * TILE_R, TILE_R), TILE_R)]
            copies.append(pltpu.make_async_copy(ref, place, sent.at[CHUNKS + slot]))
            copies[-1].start()
    edge = jnp.zeros((2 * TILE_R, LANES), jnp.bfloat16)
    for first in (BLK, 3 * BLK):
        split[1, :, first : first + LANES] = edge
        split[blocks, :, first + LANES : first + BLK] = edge

    def window(ref, halo, cols):
        tile = lambda index: ref[0, pl.ds(pl.multiple_of(index * TILE_R, TILE_R), TILE_R), cols]
        if kind == "middle":
            return [tile(0), tile(1), tile(2)]
        centre = tile(1)
        return [jnp.where(top, halo, centre), tile(2 * side), jnp.where(top, centre, halo)]

    def rows_step(block, carry):
        cols = pl.ds(pl.multiple_of(block * BLK, BLK), BLK)
        halo = [None, None] if kind == "middle" else [halo_ref[0, :, cols], halo_ref[1, :, cols]]
        weights = [tile * SHARE for tile in window(weight_ref, halo[1], cols)]
        values = [value * weight for value, weight in zip(window(cube_ref, halo[0], cols), weights)]
        for half in range(2):
            for at, tiles in ((2 * half, values), (2 * half + 1, weights)):
                for i, tile in enumerate(tiles):
                    lines[at, TILE_R * i : TILE_R * (i + 1)] = tile[:, half * LANES : (half + 1) * LANES]
        halves = []
        for half in range(2):
            made = []
            for at in (2 * half, 2 * half + 1):
                line = lambda start: lines[at, start : start + TILE_R]
                total = TAPS[0] * line(RAD)
                for shift in range(1, RAD + 1):
                    total = total + TAPS[shift] * (line(RAD - shift) + line(RAD + shift))
                made.append(total)
            halves.append(jnp.concatenate(made, axis=0))
        both = jnp.concatenate(halves, axis=1)
        high = both.astype(jnp.bfloat16)
        low = (both - high.astype(jnp.float32)).astype(jnp.bfloat16)
        for part, base in ((high, 0), (low, 2 * BLK)):
            split[block + 1, :, base : base + BLK] = part
            split[block + 2, :, base + BLK : base + BLK + LANES] = part[:, LANES:]
            split[block, :, base + BLK + LANES : base + 2 * BLK] = part[:, :LANES]
        return carry

    lax.fori_loop(0, blocks, rows_step, 0, unroll=UNROLL)

    group = blocks // CHUNKS
    for step in range(CHUNKS):
        part = split[step * group + 1 : (step + 1) * group + 1].reshape(group * 2 * TILE_R, 4 * BLK)
        both = jnp.dot(part[:, : 2 * BLK], high_ref[...], preferred_element_type=jnp.float32)
        both += jnp.dot(part[:, 2 * BLK :], high_ref[...], preferred_element_type=jnp.float32)
        both += jnp.dot(part[:, : 2 * BLK], low_ref[...], preferred_element_type=jnp.float32)
        both = both.reshape(group, 2 * TILE_R, BLK)
        ratio = both[:, :TILE_R] / both[:, TILE_R:]
        first = step * (group // 2)
        for i in range(group):
            out_ref[first + i // 2, :, (i % 2) * BLK : (i % 2 + 1) * BLK] = ratio[i]
        if kind == "far":
            piece = pl.ds(first, group // 2)
            place = out_hbm.at[piece, pl.ds(pl.multiple_of(2 * side * TILE_R, TILE_R), TILE_R)]
            copies.append(pltpu.make_async_copy(out_ref.at[piece], place, sent.at[step]))
            copies[-1].start()
    for copy in copies:
        copy.wait()


def edge_kernel(side_ref, cube_ref, weight_ref, far_ref, near_ref, high_ref, low_ref, done):
    side = side_ref[0]
    columns = cube_ref.shape[2]
    last = cube_ref.shape[1] - TILE_R
    copies = []
    for k, (out_ref, start) in enumerate(((far_ref, side * last), (near_ref, (1 - side) * last))):
        rows = pl.ds(pl.multiple_of(start, TILE_R), TILE_R)
        for j, ref in enumerate((cube_ref, weight_ref)):
            place = out_ref.at[j, :, :columns]
            copies.append(pltpu.make_async_copy(ref.at[0, rows], place, done.at[2 * k + j]))
    for copy in copies:
        copy.start()
    far_ref[:, :, columns:] = jnp.zeros((2, TILE_R, LANES), jnp.float32)
    band_matrices(high_ref, low_ref)
    for copy in copies:
        copy.wait()


def edge_rows(side, cube, weight):
    columns = cube.shape[2]
    edges = [pltpu.VMEM((2, TILE_R, columns + extra), cube.dtype) for extra in (LANES, 0)]
    band = pltpu.VMEM((2 * BLK, BLK), jnp.bfloat16)
    whole = pl.BlockSpec(memory_space=pltpu.VMEM)
    return pl.pallas_call(
        edge_kernel,
        out_shape=edges + [band, band],
        in_specs=[pl.BlockSpec(memory_space=pltpu.SMEM)] + [pl.BlockSpec(memory_space=pl.ANY)] * 2,
        out_specs=[whole] * 4,
        scratch_shapes=[pltpu.SemaphoreType.DMA((4,))],
        compiler_params=pltpu.CompilerParams(vmem_limit_bytes=8 * 1024 * 1024),
        cost_estimate=pl.CostEstimate(
            flops=10**11, bytes_accessed=64 * TILE_R * columns, transcendentals=0
        ),
    )(side, cube, weight)


def smooth_rows(kind, side, cube, weight, *rest):
    columns = cube.shape[2]
    tiles = columns // TILE_C
    whole = pl.BlockSpec(memory_space=pltpu.VMEM)
    part = pltpu.VMEM((tiles, TILE_R, TILE_C), jnp.float32)
    out_shape, out_specs, scratch = part, whole, []
    if kind == "far":
        out_shape = pltpu.HBM((tiles, cube.shape[1], TILE_C), jnp.float32)
        out_specs = pl.BlockSpec(memory_space=pl.ANY)
        scratch = [part, pltpu.SemaphoreType.DMA((CHUNKS + 2,))]
    return pl.pallas_call(
        functools.partial(smooth_kernel, kind),
        out_shape=out_shape,
        in_specs=[pl.BlockSpec(memory_space=pltpu.SMEM)] + [whole] * (2 + len(rest)),
        out_specs=out_specs,
        scratch_shapes=scratch
        + [
            pltpu.VMEM((columns // BLK + 2, 2 * TILE_R, 4 * BLK), jnp.bfloat16),
            pltpu.VMEM((4, 3 * TILE_R, LANES), jnp.float32),
        ],
        compiler_params=pltpu.CompilerParams(vmem_limit_bytes=24 * 1024 * 1024),
        cost_estimate=pl.CostEstimate(flops=0, bytes_accessed=0, transcendentals=0),
    )(side, cube, weight, *rest)


def norm_kernel(smooth_ref, halo_ref, mask_ref, flags_ref, width_ref, out_hbm, out_ref, sent):
    channels, rows, columns = smooth_ref.shape
    shape = (TILE_R, LANES)
    below = jnp.broadcast_to(width_ref[0:1, :], shape)
    above = jnp.broadcast_to(width_ref[1:2, :], shape)
    keep_low = [(below >= HW - j).astype(jnp.float32) for j in range(HW)]
    keep_high = [(above > j).astype(jnp.float32) for j in range(HW)]

    def whole(x):
        return jnp.sum(jnp.sum(x, axis=1, keepdims=True), axis=0, keepdims=True)

    copies = []
    for tile in range(rows // TILE_R):
        lines = slice(tile * TILE_R, (tile + 1) * TILE_R)
        sums = [jnp.zeros((TILE_R, LANES), jnp.float32) for _ in WIDTHS]
        kept = jnp.zeros((TILE_R, LANES), jnp.float32)
        for strip in range(columns // LANES):
            cols = slice(strip * LANES, (strip + 1) * LANES)
            keep = (mask_ref[lines, cols] == 0).astype(jnp.float32)
            kept = kept + keep
            extended = [halo_ref[j, lines, cols] * keep_low[j] for j in range(HW)]
            extended += [smooth_ref[c, lines, cols] for c in range(channels)]
            extended += [halo_ref[HW + j, lines, cols] * keep_high[j] for j in range(HW)]
            squares = [jnp.zeros((TILE_R, LANES), jnp.float32) for _ in WIDTHS]
            for c in range(channels):
                at = c + HW
                total = extended[at]
                reach = 0
                for i, width in enumerate(WIDTHS):
                    while reach < width // 2:
                        reach += 1
                        total = total + (extended[at - reach] + extended[at + reach])
                    boxcar = total * (1.0 / width)
                    out_ref[i, c, lines, cols] = boxcar
                    squares[i] = squares[i] + boxcar * boxcar
            sums = [total + square * keep for total, square in zip(sums, squares)]
        count = jnp.maximum(whole(kept) * channels, 1.0)
        flag = flags_ref[tile : tile + 1, :].astype(jnp.float32)
        for i in range(len(WIDTHS)):
            factor = flag / jnp.sqrt(whole(sums[i]) / count + 1e-06)
            factor = jnp.broadcast_to(factor, (TILE_R, columns))
            for c in range(channels):
                out_ref[i, c, lines] = out_ref[i, c, lines] * factor
            copies.append(
                pltpu.make_async_copy(out_ref.at[i, :, lines], out_hbm.at[i, :, lines], sent.at[tile, i])
            )
            copies[-1].start()
    for copy in copies:
        copy.wait()


def normalize(smoothed, halo, mask, flags, widths):
    out = (len(WIDTHS),) + smoothed.shape
    whole = pl.BlockSpec(memory_space=pltpu.VMEM)
    return pl.pallas_call(
        norm_kernel,
        out_shape=jax.ShapeDtypeStruct(out, jnp.float32),
        in_specs=[whole] * 5,
        out_specs=pl.BlockSpec(memory_space=pl.ANY),
        scratch_shapes=[
            pltpu.VMEM(out, jnp.float32),
            pltpu.SemaphoreType.DMA((smoothed.shape[1] // TILE_R, len(WIDTHS))),
        ],
        compiler_params=pltpu.CompilerParams(vmem_limit_bytes=16 * 1024 * 1024),
        cost_estimate=pl.CostEstimate(
            flops=30 * smoothed.size, bytes_accessed=20 * smoothed.size, transcendentals=0
        ),
    )(smoothed, halo, mask, flags, widths)


def local(cube, noise_weight, spectral_halo, source_mask, tile_flags, halo_width):
    sky = lax.axis_size("sky")
    side = lax.axis_index("sky") & 1
    near = [(i, i ^ 1) for i in range(sky)]
    far = [(i, i + 1) for i in range(1, sky - 1, 2)]
    far = far + [(target, source) for source, target in far]
    sides = jnp.reshape(side, (1,))
    stay = [pltpu.with_memory_space_constraint(part, pltpu.HBM) for part in (cube, noise_weight)]
    far_edge, near_edge, *band = edge_rows(sides, *stay)
    far_halo = lax.ppermute(far_edge, "sky", far)
    near_halo = lax.ppermute(near_edge, "sky", near)
    middle = smooth_rows("middle", sides, cube, noise_weight, *band)
    near_part = smooth_rows("near", sides, cube, noise_weight, near_halo, *band)
    far_halo = pltpu.with_memory_space_constraint(far_halo, pltpu.VMEM)
    smoothed = smooth_rows("far", sides, cube, noise_weight, far_halo, *band, middle, near_part)
    smoothed = lax.all_to_all(smoothed, "chan", split_axis=0, concat_axis=0, tiled=True)
    return normalize(smoothed, spectral_halo, source_mask, tile_flags, halo_width)


def solution(mesh):
    placed = (
        P("chan", "sky", None),
        P("chan", "sky", None),
        P(None, "sky", "chan"),
        P("sky", "chan"),
        P("sky", "chan"),
        P(None, "chan"),
    )
    return jax.shard_map(
        local, mesh=mesh, in_specs=placed, out_specs=P(None, None, "sky", "chan"), check_vma=False
    )
```

```python
import functools
import math

import jax
import jax.numpy as jnp
from jax import lax
from jax.experimental import pallas as pl
from jax.experimental.pallas import tpu as pltpu
from jax.sharding import PartitionSpec as P

RAD = 8
HW = 4
TILE_R = 8
TILE_C = 512
BLK = 256
LANES = 128
CHUNKS = 4
UNROLL = 8
SHARE = 2.0**-7
WIDTHS = (3, 5, 9)


def tap_list():
    sigma = RAD / 2.5
    return [math.exp(-((shift - RAD) ** 2) / (2.0 * sigma * sigma)) for shift in range(2 * RAD + 1)]


TAPS = tap_list()[RAD:]


def band_matrices(high_ref, low_ref):
    shape = (LANES, BLK)
    target = lax.broadcasted_iota(jnp.int32, shape, 1)
    for part, first in enumerate((0, LANES, -LANES, BLK)):
        reach = jnp.abs(lax.broadcasted_iota(jnp.int32, shape, 0) + first - target)
        band = jnp.zeros(shape, jnp.float32)
        for shift in range(RAD + 1):
            band = jnp.where(reach == shift, TAPS[shift], band)
        high = band.astype(jnp.bfloat16)
        rows = slice(part * LANES, (part + 1) * LANES)
        high_ref[rows] = high
        low_ref[rows] = (band - high.astype(jnp.float32)).astype(jnp.bfloat16)


def smooth_kernel(kind, side_ref, cube_ref, weight_ref, *rest):
    if kind == "middle":
        high_ref, low_ref, out_ref, split, lines = rest
    elif kind == "near":
        halo_ref, high_ref, low_ref, out_ref, split, lines = rest
    else:
        halo_ref, high_ref, low_ref, middle_ref, near_ref, out_hbm, out_ref, sent, split, lines = rest
    side = 1 - side_ref[0] if kind == "near" else side_ref[0]
    top = side == 0
    blocks = cube_ref.shape[2] // BLK
    copies = []
    if kind == "far":
        for slot, (ref, tile) in enumerate(((middle_ref, 1), (near_ref, 2 * (1 - side)))):
            place = out_hbm.at[:, pl.ds(pl.multiple_of(tile * TILE_R, TILE_R), TILE_R)]
            copies.append(pltpu.make_async_copy(ref, place, sent.at[CHUNKS + slot]))
            copies[-1].start()
    edge = jnp.zeros((2 * TILE_R, LANES), jnp.bfloat16)
    for first in (BLK, 3 * BLK):
        split[1, :, first : first + LANES] = edge
        split[blocks, :, first + LANES : first + BLK] = edge

    def window(ref, halo, cols):
        tile = lambda index: ref[0, pl.ds(pl.multiple_of(index * TILE_R, TILE_R), TILE_R), cols]
        if kind == "middle":
            return [tile(0), tile(1), tile(2)]
        centre = tile(1)
        return [jnp.where(top, halo, centre), tile(2 * side), jnp.where(top, centre, halo)]

    def rows_step(block, slot):
        cols = pl.ds(pl.multiple_of(block * BLK, BLK), BLK)
        halo = [None, None] if kind == "middle" else [halo_ref[0, :, cols], halo_ref[1, :, cols]]
        weights = [tile * SHARE for tile in window(weight_ref, halo[1], cols)]
        values = [value * weight for value, weight in zip(window(cube_ref, halo[0], cols), weights)]
        for half in range(2):
            for at, tiles in ((2 * half, values), (2 * half + 1, weights)):
                for i, tile in enumerate(tiles):
                    lines[4 * slot + at, TILE_R * i : TILE_R * (i + 1)] = tile[:, half * LANES : (half + 1) * LANES]
        halves = []
        for half in range(2):
            made = []
            for at in (2 * half, 2 * half + 1):
                line = lambda start: lines[4 * slot + at, start : start + TILE_R]
                total = TAPS[0] * line(RAD)
                for shift in range(1, RAD + 1):
                    total = total + TAPS[shift] * (line(RAD - shift) + line(RAD + shift))
                made.append(total)
            halves.append(jnp.concatenate(made, axis=0))
        both = jnp.concatenate(halves, axis=1)
        high = both.astype(jnp.bfloat16)
        low = (both - high.astype(jnp.float32)).astype(jnp.bfloat16)
        for part, base in ((high, 0), (low, 2 * BLK)):
            split[block + 1, :, base : base + BLK] = part
            split[block + 2, :, base + BLK : base + BLK + LANES] = part[:, LANES:]
            split[block, :, base + BLK + LANES : base + 2 * BLK] = part[:, :LANES]

    def rows_steps(step, carry):
        for slot in range(UNROLL):
            rows_step(step * UNROLL + slot, slot)
        return carry

    lax.fori_loop(0, blocks // UNROLL, rows_steps, 0)

    group = blocks // CHUNKS
    for step in range(CHUNKS):
        part = split[step * group + 1 : (step + 1) * group + 1].reshape(group * 2 * TILE_R, 4 * BLK)
        both = jnp.dot(part[:, : 2 * BLK], high_ref[...], preferred_element_type=jnp.float32)
        both += jnp.dot(part[:, 2 * BLK :], high_ref[...], preferred_element_type=jnp.float32)
        both += jnp.dot(part[:, : 2 * BLK], low_ref[...], preferred_element_type=jnp.float32)
        both = both.reshape(group, 2 * TILE_R, BLK)
        ratio = both[:, :TILE_R] / both[:, TILE_R:]
        first = step * (group // 2)
        for i in range(group):
            out_ref[first + i // 2, :, (i % 2) * BLK : (i % 2 + 1) * BLK] = ratio[i]
        if kind == "far":
            piece = pl.ds(first, group // 2)
            place = out_hbm.at[piece, pl.ds(pl.multiple_of(2 * side * TILE_R, TILE_R), TILE_R)]
            copies.append(pltpu.make_async_copy(out_ref.at[piece], place, sent.at[step]))
            copies[-1].start()
    for copy in copies:
        copy.wait()


def edge_kernel(side_ref, cube_ref, weight_ref, far_ref, near_ref, high_ref, low_ref, done):
    side = side_ref[0]
    columns = cube_ref.shape[2]
    last = cube_ref.shape[1] - TILE_R
    copies = []
    for k, (out_ref, start) in enumerate(((far_ref, side * last), (near_ref, (1 - side) * last))):
        rows = pl.ds(pl.multiple_of(start, TILE_R), TILE_R)
        for j, ref in enumerate((cube_ref, weight_ref)):
            place = out_ref.at[j, :, :columns]
            copies.append(pltpu.make_async_copy(ref.at[0, rows], place, done.at[2 * k + j]))
    for copy in copies:
        copy.start()
    far_ref[:, :, columns:] = jnp.zeros((2, TILE_R, LANES), jnp.float32)
    band_matrices(high_ref, low_ref)
    for copy in copies:
        copy.wait()


def edge_rows(side, cube, weight):
    columns = cube.shape[2]
    edges = [pltpu.VMEM((2, TILE_R, columns + extra), cube.dtype) for extra in (LANES, 0)]
    band = pltpu.VMEM((2 * BLK, BLK), jnp.bfloat16)
    whole = pl.BlockSpec(memory_space=pltpu.VMEM)
    return pl.pallas_call(
        edge_kernel,
        out_shape=edges + [band, band],
        in_specs=[pl.BlockSpec(memory_space=pltpu.SMEM)] + [pl.BlockSpec(memory_space=pl.ANY)] * 2,
        out_specs=[whole] * 4,
        scratch_shapes=[pltpu.SemaphoreType.DMA((4,))],
        compiler_params=pltpu.CompilerParams(vmem_limit_bytes=8 * 1024 * 1024),
        cost_estimate=pl.CostEstimate(
            flops=10**11, bytes_accessed=64 * TILE_R * columns, transcendentals=0
        ),
    )(side, cube, weight)


def smooth_rows(kind, side, cube, weight, *rest):
    columns = cube.shape[2]
    tiles = columns // TILE_C
    whole = pl.BlockSpec(memory_space=pltpu.VMEM)
    part = pltpu.VMEM((tiles, TILE_R, TILE_C), jnp.float32)
    out_shape, out_specs, scratch = part, whole, []
    if kind == "far":
        out_shape = pltpu.HBM((tiles, cube.shape[1], TILE_C), jnp.float32)
        out_specs = pl.BlockSpec(memory_space=pl.ANY)
        scratch = [part, pltpu.SemaphoreType.DMA((CHUNKS + 2,))]
    return pl.pallas_call(
        functools.partial(smooth_kernel, kind),
        out_shape=out_shape,
        in_specs=[pl.BlockSpec(memory_space=pltpu.SMEM)] + [whole] * (2 + len(rest)),
        out_specs=out_specs,
        scratch_shapes=scratch
        + [
            pltpu.VMEM((columns // BLK + 2, 2 * TILE_R, 4 * BLK), jnp.bfloat16),
            pltpu.VMEM((4 * UNROLL, 3 * TILE_R, LANES), jnp.float32),
        ],
        compiler_params=pltpu.CompilerParams(vmem_limit_bytes=24 * 1024 * 1024),
        cost_estimate=pl.CostEstimate(flops=0, bytes_accessed=0, transcendentals=0),
    )(side, cube, weight, *rest)


def norm_kernel(smooth_ref, halo_ref, mask_ref, flags_ref, width_ref, out_hbm, out_ref, sent):
    channels, rows, columns = smooth_ref.shape
    shape = (TILE_R, LANES)
    below = jnp.broadcast_to(width_ref[0:1, :], shape)
    above = jnp.broadcast_to(width_ref[1:2, :], shape)
    keep_low = [(below >= HW - j).astype(jnp.float32) for j in range(HW)]
    keep_high = [(above > j).astype(jnp.float32) for j in range(HW)]

    def whole(x):
        return jnp.sum(jnp.sum(x, axis=1, keepdims=True), axis=0, keepdims=True)

    copies = []
    for tile in range(rows // TILE_R):
        lines = slice(tile * TILE_R, (tile + 1) * TILE_R)
        sums = [jnp.zeros((TILE_R, LANES), jnp.float32) for _ in WIDTHS]
        kept = jnp.zeros((TILE_R, LANES), jnp.float32)
        for strip in range(columns // LANES):
            cols = slice(strip * LANES, (strip + 1) * LANES)
            keep = (mask_ref[lines, cols] == 0).astype(jnp.float32)
            kept = kept + keep
            extended = [halo_ref[j, lines, cols] * keep_low[j] for j in range(HW)]
            extended += [smooth_ref[c, lines, cols] for c in range(channels)]
            extended += [halo_ref[HW + j, lines, cols] * keep_high[j] for j in range(HW)]
            squares = [jnp.zeros((TILE_R, LANES), jnp.float32) for _ in WIDTHS]
            threes = [a + b + c for a, b, c in zip(extended, extended[1:], extended[2:])]
            for c in range(channels):
                three = threes[c + HW - 1]
                five = three + (extended[c + HW - 2] + extended[c + HW + 2])
                nine = three + (threes[c + HW - 4] + threes[c + HW + 2])
                for i, (total, width) in enumerate(zip((three, five, nine), WIDTHS)):
                    boxcar = total * (1.0 / width)
                    out_ref[i, c, lines, cols] = boxcar
                    squares[i] = squares[i] + boxcar * boxcar
            sums = [total + square * keep for total, square in zip(sums, squares)]
        count = jnp.maximum(whole(kept) * channels, 1.0)
        flag = flags_ref[tile : tile + 1, :].astype(jnp.float32)
        for i in range(len(WIDTHS)):
            factor = flag / jnp.sqrt(whole(sums[i]) / count + 1e-06)
            factor = jnp.broadcast_to(factor, (TILE_R, columns))
            for c in range(channels):
                out_ref[i, c, lines] = out_ref[i, c, lines] * factor
            copies.append(
                pltpu.make_async_copy(out_ref.at[i, :, lines], out_hbm.at[i, :, lines], sent.at[tile, i])
            )
            copies[-1].start()
    for copy in copies:
        copy.wait()


def normalize(smoothed, halo, mask, flags, widths):
    out = (len(WIDTHS),) + smoothed.shape
    whole = pl.BlockSpec(memory_space=pltpu.VMEM)
    return pl.pallas_call(
        norm_kernel,
        out_shape=jax.ShapeDtypeStruct(out, jnp.float32),
        in_specs=[whole] * 5,
        out_specs=pl.BlockSpec(memory_space=pl.ANY),
        scratch_shapes=[
            pltpu.VMEM(out, jnp.float32),
            pltpu.SemaphoreType.DMA((smoothed.shape[1] // TILE_R, len(WIDTHS))),
        ],
        compiler_params=pltpu.CompilerParams(vmem_limit_bytes=16 * 1024 * 1024),
        cost_estimate=pl.CostEstimate(
            flops=30 * smoothed.size, bytes_accessed=20 * smoothed.size, transcendentals=0
        ),
    )(smoothed, halo, mask, flags, widths)


def local(cube, noise_weight, spectral_halo, source_mask, tile_flags, halo_width):
    sky = lax.axis_size("sky")
    side = lax.axis_index("sky") & 1
    near = [(i, i ^ 1) for i in range(sky)]
    far = [(i, i + 1) for i in range(1, sky - 1, 2)]
    far = far + [(target, source) for source, target in far]
    sides = jnp.reshape(side, (1,))
    stay = [pltpu.with_memory_space_constraint(part, pltpu.HBM) for part in (cube, noise_weight)]
    far_edge, near_edge, *band = edge_rows(sides, *stay)
    far_halo = lax.ppermute(far_edge, "sky", far)
    near_halo = lax.ppermute(near_edge, "sky", near)
    middle = smooth_rows("middle", sides, cube, noise_weight, *band)
    near_part = smooth_rows("near", sides, cube, noise_weight, near_halo, *band)
    far_halo = pltpu.with_memory_space_constraint(far_halo, pltpu.VMEM)
    smoothed = smooth_rows("far", sides, cube, noise_weight, far_halo, *band, middle, near_part)
    smoothed = lax.all_to_all(smoothed, "chan", split_axis=0, concat_axis=0, tiled=True)
    return normalize(smoothed, spectral_halo, source_mask, tile_flags, halo_width)


def solution(mesh):
    placed = (
        P("chan", "sky", None),
        P("chan", "sky", None),
        P(None, "sky", "chan"),
        P("sky", "chan"),
        P("sky", "chan"),
        P(None, "chan"),
    )
    return jax.shard_map(
        local, mesh=mesh, in_specs=placed, out_specs=P(None, None, "sky", "chan"), check_vma=False
    )
```

```python
import functools
import math

import jax
import jax.numpy as jnp
from jax import lax
from jax.experimental import pallas as pl
from jax.experimental.pallas import tpu as pltpu
from jax.sharding import PartitionSpec as P

RAD = 8
HW = 4
TILE_R = 8
TILE_C = 512
BLK = 256
LANES = 128
CHUNKS = 4
UNROLL = 8
SHARE = 2.0**-7
WIDTHS = (3, 5, 9)


def tap_list():
    sigma = RAD / 2.5
    return [math.exp(-((shift - RAD) ** 2) / (2.0 * sigma * sigma)) for shift in range(2 * RAD + 1)]


TAPS = tap_list()[RAD:]


def band_matrices(high_ref, low_ref):
    shape = (LANES, BLK)
    target = lax.broadcasted_iota(jnp.int32, shape, 1)
    for part, first in enumerate((0, LANES, -LANES, BLK)):
        reach = jnp.abs(lax.broadcasted_iota(jnp.int32, shape, 0) + first - target)
        band = jnp.zeros(shape, jnp.float32)
        for shift in range(RAD + 1):
            band = jnp.where(reach == shift, TAPS[shift], band)
        high = band.astype(jnp.bfloat16)
        rows = slice(part * LANES, (part + 1) * LANES)
        high_ref[rows] = high
        low_ref[rows] = (band - high.astype(jnp.float32)).astype(jnp.bfloat16)


def smooth_kernel(kind, cube_ref, weight_ref, *rest):
    if kind == "middle":
        high_ref, low_ref, out_ref, split, lines = rest
    elif kind == "near":
        halo_ref, high_ref, low_ref, out_ref, split, lines = rest
    else:
        halo_ref, high_ref, low_ref, middle_ref, near_ref, out_hbm, out_ref, sent, split, lines = rest
    side = lax.axis_index("sky") & 1
    side = 1 - side if kind == "near" else side
    top = side == 0
    blocks = cube_ref.shape[2] // BLK
    copies = []
    if kind == "far":
        for slot, (ref, tile) in enumerate(((middle_ref, 1), (near_ref, 2 * (1 - side)))):
            place = out_hbm.at[:, pl.ds(pl.multiple_of(tile * TILE_R, TILE_R), TILE_R)]
            copies.append(pltpu.make_async_copy(ref, place, sent.at[CHUNKS + slot]))
            copies[-1].start()
    edge = jnp.zeros((2 * TILE_R, LANES), jnp.bfloat16)
    for first in (BLK, 3 * BLK):
        split[1, :, first : first + LANES] = edge
        split[blocks, :, first + LANES : first + BLK] = edge

    def window(ref, halo, cols):
        tile = lambda index: ref[0, pl.ds(pl.multiple_of(index * TILE_R, TILE_R), TILE_R), cols]
        if kind == "middle":
            return [tile(0), tile(1), tile(2)]
        centre = tile(1)
        return [jnp.where(top, halo, centre), tile(2 * side), jnp.where(top, centre, halo)]

    def rows_step(block, slot):
        cols = pl.ds(pl.multiple_of(block * BLK, BLK), BLK)
        halo = [None, None] if kind == "middle" else [halo_ref[0, :, cols], halo_ref[1, :, cols]]
        weights = [tile * SHARE for tile in window(weight_ref, halo[1], cols)]
        values = [value * weight for value, weight in zip(window(cube_ref, halo[0], cols), weights)]
        for half in range(2):
            for at, tiles in ((2 * half, values), (2 * half + 1, weights)):
                for i, tile in enumerate(tiles):
                    lines[4 * slot + at, TILE_R * i : TILE_R * (i + 1)] = tile[:, half * LANES : (half + 1) * LANES]
        halves = []
        for half in range(2):
            made = []
            for at in (2 * half, 2 * half + 1):
                line = lambda start: lines[4 * slot + at, start : start + TILE_R]
                total = TAPS[0] * line(RAD)
                for shift in range(1, RAD + 1):
                    total = total + TAPS[shift] * (line(RAD - shift) + line(RAD + shift))
                made.append(total)
            halves.append(jnp.concatenate(made, axis=0))
        both = jnp.concatenate(halves, axis=1)
        high = both.astype(jnp.bfloat16)
        low = (both - high.astype(jnp.float32)).astype(jnp.bfloat16)
        for part, base in ((high, 0), (low, 2 * BLK)):
            split[block + 1, :, base : base + BLK] = part
            split[block + 2, :, base + BLK : base + BLK + LANES] = part[:, LANES:]
            split[block, :, base + BLK + LANES : base + 2 * BLK] = part[:, :LANES]

    def rows_steps(step, carry):
        for slot in range(UNROLL):
            rows_step(step * UNROLL + slot, slot)
        return carry

    lax.fori_loop(0, blocks // UNROLL, rows_steps, 0)

    group = blocks // CHUNKS
    for step in range(CHUNKS):
        part = split[step * group + 1 : (step + 1) * group + 1].reshape(group * 2 * TILE_R, 4 * BLK)
        both = jnp.dot(part[:, : 2 * BLK], high_ref[...], preferred_element_type=jnp.float32)
        both += jnp.dot(part[:, 2 * BLK :], high_ref[...], preferred_element_type=jnp.float32)
        both += jnp.dot(part[:, : 2 * BLK], low_ref[...], preferred_element_type=jnp.float32)
        both = both.reshape(group, 2 * TILE_R, BLK)
        ratio = both[:, :TILE_R] / both[:, TILE_R:]
        first = step * (group // 2)
        for i in range(group):
            out_ref[first + i // 2, :, (i % 2) * BLK : (i % 2 + 1) * BLK] = ratio[i]
        if kind == "far":
            piece = pl.ds(first, group // 2)
            place = out_hbm.at[piece, pl.ds(pl.multiple_of(2 * side * TILE_R, TILE_R), TILE_R)]
            copies.append(pltpu.make_async_copy(out_ref.at[piece], place, sent.at[step]))
            copies[-1].start()
    for copy in copies:
        copy.wait()


def edge_kernel(cube_ref, weight_ref, far_ref, near_ref, high_ref, low_ref, done):
    side = lax.axis_index("sky") & 1
    columns = cube_ref.shape[2]
    last = cube_ref.shape[1] - TILE_R
    copies = []
    for k, (out_ref, start) in enumerate(((far_ref, side * last), (near_ref, (1 - side) * last))):
        rows = pl.ds(pl.multiple_of(start, TILE_R), TILE_R)
        for j, ref in enumerate((cube_ref, weight_ref)):
            place = out_ref.at[j, :, :columns]
            copies.append(pltpu.make_async_copy(ref.at[0, rows], place, done.at[2 * k + j]))
    for copy in copies:
        copy.start()
    far_ref[:, :, columns:] = jnp.zeros((2, TILE_R, LANES), jnp.float32)
    band_matrices(high_ref, low_ref)
    for copy in copies:
        copy.wait()


def edge_rows(cube, weight):
    columns = cube.shape[2]
    edges = [pltpu.VMEM((2, TILE_R, columns + extra), cube.dtype) for extra in (LANES, 0)]
    band = pltpu.VMEM((2 * BLK, BLK), jnp.bfloat16)
    whole = pl.BlockSpec(memory_space=pltpu.VMEM)
    return pl.pallas_call(
        edge_kernel,
        out_shape=edges + [band, band],
        in_specs=[pl.BlockSpec(memory_space=pl.ANY)] * 2,
        out_specs=[whole] * 4,
        scratch_shapes=[pltpu.SemaphoreType.DMA((4,))],
        compiler_params=pltpu.CompilerParams(vmem_limit_bytes=8 * 1024 * 1024),
        cost_estimate=pl.CostEstimate(
            flops=10**11, bytes_accessed=64 * TILE_R * columns, transcendentals=0
        ),
    )(cube, weight)


def smooth_rows(kind, cube, weight, *rest):
    columns = cube.shape[2]
    tiles = columns // TILE_C
    whole = pl.BlockSpec(memory_space=pltpu.VMEM)
    part = pltpu.VMEM((tiles, TILE_R, TILE_C), jnp.float32)
    out_shape, out_specs, scratch = part, whole, []
    if kind == "far":
        out_shape = pltpu.HBM((tiles, cube.shape[1], TILE_C), jnp.float32)
        out_specs = pl.BlockSpec(memory_space=pl.ANY)
        scratch = [part, pltpu.SemaphoreType.DMA((CHUNKS + 2,))]
    return pl.pallas_call(
        functools.partial(smooth_kernel, kind),
        out_shape=out_shape,
        in_specs=[whole] * (2 + len(rest)),
        out_specs=out_specs,
        scratch_shapes=scratch
        + [
            pltpu.VMEM((columns // BLK + 2, 2 * TILE_R, 4 * BLK), jnp.bfloat16),
            pltpu.VMEM((4 * UNROLL, 3 * TILE_R, LANES), jnp.float32),
        ],
        compiler_params=pltpu.CompilerParams(vmem_limit_bytes=24 * 1024 * 1024),
        cost_estimate=pl.CostEstimate(flops=0, bytes_accessed=0, transcendentals=0),
    )(cube, weight, *rest)


def norm_kernel(smooth_ref, halo_ref, mask_ref, flags_ref, width_ref, out_hbm, out_ref, sent):
    channels, rows, columns = smooth_ref.shape
    shape = (TILE_R, LANES)
    below = jnp.broadcast_to(width_ref[0:1, :], shape)
    above = jnp.broadcast_to(width_ref[1:2, :], shape)
    keep_low = [(below >= HW - j).astype(jnp.float32) for j in range(HW)]
    keep_high = [(above > j).astype(jnp.float32) for j in range(HW)]

    def whole(x):
        return jnp.sum(jnp.sum(x, axis=1, keepdims=True), axis=0, keepdims=True)

    copies = []
    for tile in range(rows // TILE_R):
        lines = slice(tile * TILE_R, (tile + 1) * TILE_R)
        sums = [jnp.zeros((TILE_R, LANES), jnp.float32) for _ in WIDTHS]
        kept = jnp.zeros((TILE_R, LANES), jnp.float32)
        for strip in range(columns // LANES):
            cols = slice(strip * LANES, (strip + 1) * LANES)
            keep = (mask_ref[lines, cols] == 0).astype(jnp.float32)
            kept = kept + keep
            extended = [halo_ref[j, lines, cols] * keep_low[j] for j in range(HW)]
            extended += [smooth_ref[c, lines, cols] for c in range(channels)]
            extended += [halo_ref[HW + j, lines, cols] * keep_high[j] for j in range(HW)]
            squares = [jnp.zeros((TILE_R, LANES), jnp.float32) for _ in WIDTHS]
            threes = [a + b + c for a, b, c in zip(extended, extended[1:], extended[2:])]
            for c in range(channels):
                three = threes[c + HW - 1]
                five = three + (extended[c + HW - 2] + extended[c + HW + 2])
                nine = three + (threes[c + HW - 4] + threes[c + HW + 2])
                for i, (total, width) in enumerate(zip((three, five, nine), WIDTHS)):
                    boxcar = total * (1.0 / width)
                    out_ref[i, c, lines, cols] = boxcar
                    squares[i] = squares[i] + boxcar * boxcar
            sums = [total + square * keep for total, square in zip(sums, squares)]
        count = jnp.maximum(whole(kept) * channels, 1.0)
        flag = flags_ref[tile : tile + 1, :].astype(jnp.float32)
        for i in range(len(WIDTHS)):
            factor = flag / jnp.sqrt(whole(sums[i]) / count + 1e-06)
            factor = jnp.broadcast_to(factor, (TILE_R, columns))
            for c in range(channels):
                out_ref[i, c, lines] = out_ref[i, c, lines] * factor
            copies.append(
                pltpu.make_async_copy(out_ref.at[i, :, lines], out_hbm.at[i, :, lines], sent.at[tile, i])
            )
            copies[-1].start()
    for copy in copies:
        copy.wait()


def normalize(smoothed, halo, mask, flags, widths):
    out = (len(WIDTHS),) + smoothed.shape
    whole = pl.BlockSpec(memory_space=pltpu.VMEM)
    return pl.pallas_call(
        norm_kernel,
        out_shape=jax.ShapeDtypeStruct(out, jnp.float32),
        in_specs=[whole] * 5,
        out_specs=pl.BlockSpec(memory_space=pl.ANY),
        scratch_shapes=[
            pltpu.VMEM(out, jnp.float32),
            pltpu.SemaphoreType.DMA((smoothed.shape[1] // TILE_R, len(WIDTHS))),
        ],
        compiler_params=pltpu.CompilerParams(vmem_limit_bytes=16 * 1024 * 1024),
        cost_estimate=pl.CostEstimate(
            flops=30 * smoothed.size, bytes_accessed=20 * smoothed.size, transcendentals=0
        ),
    )(smoothed, halo, mask, flags, widths)


def local(cube, noise_weight, spectral_halo, source_mask, tile_flags, halo_width):
    sky = lax.axis_size("sky")
    near = [(i, i ^ 1) for i in range(sky)]
    far = [(i, i + 1) for i in range(1, sky - 1, 2)]
    far = far + [(target, source) for source, target in far]
    stay = [pltpu.with_memory_space_constraint(part, pltpu.HBM) for part in (cube, noise_weight)]
    far_edge, near_edge, *band = edge_rows(*stay)
    far_halo = lax.ppermute(far_edge, "sky", far)
    near_halo = lax.ppermute(near_edge, "sky", near)
    middle = smooth_rows("middle", cube, noise_weight, *band)
    near_part = smooth_rows("near", cube, noise_weight, near_halo, *band)
    far_halo = pltpu.with_memory_space_constraint(far_halo, pltpu.VMEM)
    smoothed = smooth_rows("far", cube, noise_weight, far_halo, *band, middle, near_part)
    smoothed = lax.all_to_all(smoothed, "chan", split_axis=0, concat_axis=0, tiled=True)
    return normalize(smoothed, spectral_halo, source_mask, tile_flags, halo_width)


def solution(mesh):
    placed = (
        P("chan", "sky", None),
        P("chan", "sky", None),
        P(None, "sky", "chan"),
        P("sky", "chan"),
        P("sky", "chan"),
        P(None, "chan"),
    )
    return jax.shard_map(
        local, mesh=mesh, in_specs=placed, out_specs=P(None, None, "sky", "chan"), check_vma=False
    )
```
